128 devices in a mesh: dp: 4 (over z), ctx: 32 (over x, y, core).
Axes of the slice: x: 4, y: 4, z: 4, core: 2. Of those that a mesh axis runs over, the one named last changes fastest.
Arguments:
- queries: bfloat16 [4, 4096, 3072], P('dp', 'ctx'), may hold values from -48 to 48
- key_rows: bfloat16 [4, 4096, 512], P('dp', 'ctx'), may hold values from -6 to 6
- value_rows: bfloat16 [4, 4096, 512], P('dp', 'ctx'), may hold values from -6 to 6
- upstream: bfloat16 [4, 4096, 3072], P('dp', 'ctx'), may hold values from -6 to 6
- loss_weight: float32 [4, 4096], P('dp', 'ctx'), may hold values from 0.25 to 12
- doc_lengths: int32 [4, 8], P('dp'), may hold values from 1 to 2048, 4096 in all within a row
Outputs:
- attended: bfloat16 [4, 4096, 3072], P('dp', 'ctx')
- query_grad: bfloat16 [4, 4096, 3072], P('dp', 'ctx')
- key_grad: bfloat16 [4, 4096, 512], P('dp', 'ctx')
- value_grad: bfloat16 [4, 4096, 512], P('dp', 'ctx')
The draws below stay inside these ranges and needn't reach their ends.
Inputs may be any that keep to these rules, and one draw needn't show every extreme that they name: `doc_lengths`: each row holds 8 lengths that sum to 4096; the largest is exactly 2048.
All inputs are finite; a program needn't handle non-finite values.
Results may differ from the reference program's by a relative error of at most 0.025.
Values may be sent and summed in bfloat16 or wider, within the bound.
No kernel may reach another device: no remote copies, remote signals or barrier semaphores. Data moves between devices by JAX's collectives and lax.ppermute only.
A program may use at most 128 MiB of HBM per device.

```python
import math
import jax
import jax.numpy as jnp
import numpy as np
from jax import lax

QH = 24
KVH = 4
HD = 128
NDOC = 8
SEQS = 4
LEN = 4096
MOST = 2048


def draw_loss_weight(key, part):
    key = jax.random.fold_in(key, 7)
    base = jax.random.uniform(key, (SEQS, LEN), jnp.float32)
    ramp = 1.0 + 2.0 * jnp.arange(SEQS * LEN, dtype=jnp.float32).reshape(SEQS, LEN) / (SEQS * LEN - 1)
    return jnp.exp(jnp.log(0.5) + base * jnp.log(8.0)) * ramp


def draw_queries(key, part):
    key = jax.random.fold_in(key, 11)
    entry_key = jax.random.fold_in(key, 1)
    factor_key = jax.random.fold_in(key, 2)
    spread = jax.random.uniform(factor_key, (SEQS, LEN, 1), jnp.float32)
    entries = jnp.clip(jax.random.normal(entry_key, (SEQS, LEN, QH * HD), jnp.float32), -6.0, 6.0)
    factor = jnp.exp(spread * jnp.log(8.0))
    return (entries * factor).astype(jnp.bfloat16)


def levels(rng, shape, pieces, smallest, high):
    loudness, own = 1.0, jax.random.fold_in(rng, 6)
    for axis_at, blocks in pieces:
        draws = jnp.exp(jax.random.uniform(jax.random.fold_in(own, axis_at), (blocks,), jnp.float32, smallest / len(pieces), high / len(pieces)))
        loudness = loudness * jnp.repeat(draws, shape[axis_at] // blocks).reshape([-1 if axis == axis_at else 1 for axis in range(len(shape))])
    return loudness


def profile(number_of, total, most, skew):
    weights = [(1 << 20) // math.isqrt(standing ** skew) + 1 for standing in range(2, number_of + 1)]
    spare, holding = total - most - (number_of - 1), [1] * (number_of - 1)
    while spare > 0:
        free = [i for i in range(number_of - 1) if holding[i] < most]
        pool, left = sum([weights[i] for i in free]), spare
        for i in free:
            extra = min(most - holding[i], max(1, left * weights[i] // pool), spare)
            holding[i] = holding[i] + extra
            spare = spare - extra
    return np.array([most] + holding)


def uneven_parts(stream_key, number_of, total, bound, skew):
    if number_of == 2:
        one = jax.random.randint(stream_key, (), max(1, total - bound), min(bound, total - 1) + 1)
        return jnp.stack([one, total - one])
    sizes = jnp.asarray(profile(number_of, total, bound, skew), jnp.int32)
    pairs = (number_of - 1) // 2
    giver, receiver = sizes[1:1 + 2 * pairs:2], sizes[2:2 + 2 * pairs:2]
    room = jnp.minimum(giver - 1, bound - receiver)
    moved = jax.random.randint(jax.random.fold_in(stream_key, 1), (pairs,), 0, 1 << 20) % (room + 1)
    sizes = sizes.at[1:1 + 2 * pairs:2].set(giver - moved).at[2:2 + 2 * pairs:2].set(receiver + moved)
    return sizes[jax.random.permutation(jax.random.fold_in(stream_key, 2), number_of)]


def noise(rng, dims, scale, bound, cuts=(), held_as=jnp.bfloat16):
    values = scale * jax.random.normal(rng, dims, jnp.float32)
    if cuts:
        values = values * levels(rng, dims, cuts, -0.22, 0.18)
    return jnp.clip(values, -bound, bound).astype(held_as)


def setup_inputs(seed: int = 0) -> dict:
    keys = jax.random.split(jax.random.key(seed), 7)
    return {
        "queries": draw_queries(jax.random.fold_in(keys[6], 71), 0),
        "key_rows": noise(keys[1], (SEQS, LEN, KVH * HD), 1.0, 6.0, ((0, 4), (1, 32))),
        "value_rows": noise(keys[2], (SEQS, LEN, KVH * HD), 1.0, 6.0, ((0, 4), (1, 32))),
        "upstream": noise(keys[3], (SEQS, LEN, QH * HD), 1.0, 6.0, ((0, 4), (1, 32))),
        "loss_weight": draw_loss_weight(jax.random.fold_in(keys[6], 71), 0),
        "doc_lengths": jax.vmap(lambda own: uneven_parts(own, NDOC, LEN, MOST, 2))(jax.random.split(keys[5], SEQS)).reshape((SEQS, NDOC)).astype(jnp.int32),
    }


logit_cap = 30.0


def rounded(values_in):
    return lax.optimization_barrier(values_in.astype(jnp.bfloat16)).astype(jnp.float32)


def doc_index(positions, lengths_row):
    boundary = jnp.cumsum(lengths_row.astype(jnp.int32))
    return jnp.sum((positions[:, None] >= boundary[None, :]).astype(jnp.int32), axis=1)


def reference(queries, key_rows, value_rows, upstream, loss_weight, doc_lengths):
    weight_sum = jnp.sum(loss_weight)
    score_scale = HD ** -0.5
    group_size = QH // KVH
    length = LEN
    key_block = min(length, 512)
    positions = jnp.arange(length, dtype=jnp.int32)
    out_list, dq_list, dk_list, dv_list = [], [], [], []
    for seq_row in range(SEQS):
        doc_ids = doc_index(positions, doc_lengths[seq_row])
        keys_all = key_rows[seq_row].astype(jnp.float32).reshape(length, KVH, HD)
        values_all = value_rows[seq_row].astype(jnp.float32).reshape(length, KVH, HD)
        cotangent = (upstream[seq_row].astype(jnp.float32) * (loss_weight[seq_row] / weight_sum)[:, None]).astype(jnp.bfloat16)
        queries_row = queries[seq_row]

        def advance(state_now, block_number):
            dk_sum, dv_sum = state_now
            offset = block_number * key_block
            query_blk = lax.dynamic_slice_in_dim(queries_row, offset, key_block, 0).astype(jnp.float32).reshape(key_block, KVH, group_size, HD)
            grad_blk = lax.dynamic_slice_in_dim(cotangent, offset, key_block, 0).astype(jnp.float32).reshape(key_block, KVH, group_size, HD)
            query_pos = offset + jnp.arange(key_block, dtype=jnp.int32)
            query_doc = lax.dynamic_slice_in_dim(doc_ids, offset, key_block, 0)
            allowed = (query_doc[:, None] == doc_ids[None, :]) & (positions[None, :] <= query_pos[:, None])
            raw = jnp.einsum("rhgd,bhd->hgrb", query_blk, keys_all) * score_scale
            squashed = jnp.tanh(raw / logit_cap)
            expo = jnp.where(allowed[None, None], jnp.exp(logit_cap * squashed - logit_cap), 0.0)
            denominator = jnp.sum(expo, axis=-1)
            weighted = jnp.einsum("hgrb,bhd->rhgd", rounded(expo), values_all)
            out_blk = (weighted / jnp.transpose(denominator, (2, 0, 1))[..., None]).astype(jnp.bfloat16)
            row_dot = jnp.transpose(jnp.sum(grad_blk * out_blk.astype(jnp.float32), axis=-1), (1, 2, 0))
            probs = expo / denominator[..., None]
            grad_prob = jnp.einsum("rhgd,bhd->hgrb", grad_blk, values_all)
            grad_score = rounded(probs * (grad_prob - row_dot[..., None]) * (1.0 - squashed * squashed))
            dq_blk = (jnp.einsum("hgrb,bhd->rhgd", grad_score, keys_all) * score_scale).astype(jnp.bfloat16)
            dk_sum = dk_sum + jnp.einsum("hgrb,rhgd->bhd", grad_score, query_blk) * score_scale
            dv_sum = dv_sum + jnp.einsum("hgrb,rhgd->bhd", rounded(probs), grad_blk)
            return (dk_sum, dv_sum), (out_blk.reshape(key_block, QH * HD), dq_blk.reshape(key_block, QH * HD))

        zeros_kv = jnp.zeros((length, KVH, HD), jnp.float32)
        (dk_sum, dv_sum), (out_rows, dq_rows) = lax.scan(advance, (zeros_kv, zeros_kv), jnp.arange(length // key_block, dtype=jnp.int32))
        out_list.append(out_rows.reshape(length, QH * HD))
        dq_list.append(dq_rows.reshape(length, QH * HD))
        dk_list.append(dk_sum.reshape(length, KVH * HD).astype(jnp.bfloat16))
        dv_list.append(dv_sum.reshape(length, KVH * HD).astype(jnp.bfloat16))
    return (jnp.stack(out_list), jnp.stack(dq_list), jnp.stack(dk_list), jnp.stack(dv_list))
```

```python
import functools
import math

import jax
import jax.numpy as jnp
from jax import lax
from jax.experimental import pallas as pl
from jax.experimental.pallas import tpu as pltpu
from jax.sharding import Mesh, PartitionSpec as P

QH = 24
KVH = 4
HD = 128
CAP = 30.0
NEAR = 2
GROUP = QH // KVH
ROWS = 256
HALF = 128
WIDE = GROUP * ROWS
SLOTS = 9
BF = jnp.bfloat16
F32 = jnp.float32
SCALE = HD ** (-0.5)


def dot(a, b):
    return jnp.dot(a, b, preferred_element_type=F32)


def attention_kernel(
    at_ref, len_ref, ws_ref, qm_ref, qo_ref, gm_ref, go_ref, kv_ref,
    att_ref, dq_ref, dkv_ref,
    qt, qs, gt, gs, expo, slope, out_t, dq_t, den, row_dot, ds_buf,
):
    chip = at_ref[0]
    core = at_ref[1]
    lane = lax.broadcasted_iota(jnp.int32, (1, ROWS), 1)
    flip = jnp.where(lane < HALF, core * HALF, (1 - core) * HALF - HALF)
    row_pos = chip * ROWS + lane + flip
    sub = lax.broadcasted_iota(jnp.int32, (ROWS, 1), 0)
    key_off = sub + jnp.where(sub < HALF, core * HALF, (1 - core) * HALF - HALF)

    start = jnp.zeros((1, ROWS), jnp.int32)
    low = jnp.int32(0)
    high = jnp.int32(0)
    edge = jnp.int32(0)
    for j in range(8):
        edge = edge + len_ref[j]
        start = jnp.maximum(start, jnp.where(row_pos >= edge, edge, 0))
        low = jnp.maximum(low, jnp.where(chip * ROWS >= edge, edge, 0))
        high = jnp.maximum(high, jnp.where(chip * ROWS + ROWS - 1 >= edge, edge, 0))

    for h in range(NEAR):
        for j in range(GROUP):
            for part, (q_in, g_in) in enumerate(((qm_ref, gm_ref), (qo_ref, go_ref))):
                cols = slice((h * GROUP + j) * HD, (h * GROUP + j + 1) * HD)
                rows = slice(j * ROWS + part * HALF, j * ROWS + (part + 1) * HALF)
                tile = q_in[:, cols]
                qs[h, rows, :] = tile
                qt[h, :, rows] = tile.T
                gt[h, :, rows] = g_in[:, cols].T
    out_t[...] = jnp.zeros_like(out_t)
    dq_t[...] = jnp.zeros_like(dq_t)
    den[...] = jnp.zeros_like(den)

    def forward(slot, masked):
        block = chip - slot
        for h in range(NEAR):
            keys = kv_ref[slot, :, h * HD:(h + 1) * HD]
            values_t = kv_ref[slot, :, (NEAR + h) * HD:(NEAR + h + 1) * HD].T
            for j in range(GROUP):
                cols = slice(j * ROWS, (j + 1) * ROWS)
                sq = jnp.tanh(dot(keys, qt[h, :, cols]) * (SCALE / CAP))
                e = jnp.exp2(sq * (CAP / math.log(2.0)))
                if masked:
                    key_pos = block * ROWS + key_off
                    e = jnp.where((key_pos >= start) & (key_pos <= row_pos), e, 0.0)
                eb = e.astype(BF)
                expo[slot, h, :, cols] = eb
                slope[slot, h, :, cols] = (e * (1.0 - sq * sq)).astype(BF)
                den[h, :, cols] += jnp.sum(e.reshape(ROWS // 8, 8, ROWS), axis=0)
                out_t[h, :, cols] += dot(values_t, eb)

    def needed(slot):
        return (slot <= chip) & ((chip - slot + 1) * ROWS > low)

    def forward_step(slot, carry):
        plain = (slot > 0) & ((chip - slot) * ROWS >= high)

        @pl.when(needed(slot) & plain)
        def _():
            forward(slot, False)

        @pl.when(needed(slot) & jnp.logical_not(plain))
        def _():
            forward(slot, True)

        return carry

    lax.fori_loop(0, SLOTS, forward_step, 0)

    inv_ws = 1.0 / ws_ref[0]
    for h in range(NEAR):
        for j in range(GROUP):
            cols = slice(j * ROWS, (j + 1) * ROWS)
            inv = 1.0 / jnp.sum(den[h, :, cols], axis=0, keepdims=True)
            out = (out_t[h, :, cols] * inv).astype(BF)
            hd = slice((h * GROUP + j) * HD, (h * GROUP + j + 1) * HD)
            att_ref[:, hd] = out.T
            g = (gt[h, :, cols].astype(F32) * (inv * inv_ws)).astype(BF)
            gt[h, :, cols] = g
            gs[h, cols, :] = g.T
            row_dot[h, :, cols] = jnp.sum(g.astype(F32) * out.astype(F32), axis=0, keepdims=True)

    def backward(slot):
        for h in range(NEAR):
            keys_t = kv_ref[slot, :, h * HD:(h + 1) * HD].T
            values = kv_ref[slot, :, (NEAR + h) * HD:(NEAR + h + 1) * HD]
            for j in range(GROUP):
                cols = slice(j * ROWS, (j + 1) * ROWS)
                dp = dot(values, gt[h, :, cols])
                ds = (slope[slot, h, :, cols].astype(F32) * (dp - row_dot[h, :, cols])).astype(BF)
                ds_buf[h, :, cols] = ds
                dq_t[h, :, cols] += dot(keys_t, ds)
            dkv_ref[slot, :, h * HD:(h + 1) * HD] = (dot(ds_buf[h], qs[h]) * SCALE).astype(BF)
            dkv_ref[slot, :, (NEAR + h) * HD:(NEAR + h + 1) * HD] = dot(expo[slot, h], gs[h]).astype(BF)

    def backward_step(slot, carry):
        @pl.when(needed(slot))
        def _():
            backward(slot)

        @pl.when(jnp.logical_not(needed(slot)))
        def _():
            dkv_ref[slot] = jnp.zeros((ROWS, 2 * NEAR * HD), BF)

        return carry

    lax.fori_loop(0, SLOTS, backward_step, 0)

    for h in range(NEAR):
        for j in range(GROUP):
            cols = slice(j * ROWS, (j + 1) * ROWS)
            hd = slice((h * GROUP + j) * HD, (h * GROUP + j + 1) * HD)
            dq_ref[:, hd] = (dq_t[h, :, cols] * SCALE).astype(BF).T


def attention(at, lengths, ws, qm, qo, gm, go, kv):
    smem = pl.BlockSpec(memory_space=pltpu.SMEM)
    vmem = pl.BlockSpec(memory_space=pltpu.VMEM)
    return pl.pallas_call(
        attention_kernel,
        out_shape=(
            jax.ShapeDtypeStruct((ROWS, NEAR * GROUP * HD), BF),
            jax.ShapeDtypeStruct((ROWS, NEAR * GROUP * HD), BF),
            jax.ShapeDtypeStruct((SLOTS, ROWS, 2 * NEAR * HD), BF),
        ),
        in_specs=[smem] * 3 + [vmem] * 5,
        out_specs=(vmem,) * 3,
        scratch_shapes=[
            pltpu.VMEM((NEAR, HD, WIDE), BF),
            pltpu.VMEM((NEAR, WIDE, HD), BF),
            pltpu.VMEM((NEAR, HD, WIDE), BF),
            pltpu.VMEM((NEAR, WIDE, HD), BF),
            pltpu.VMEM((SLOTS, NEAR, ROWS, WIDE), BF),
            pltpu.VMEM((SLOTS, NEAR, ROWS, WIDE), BF),
            pltpu.VMEM((NEAR, HD, WIDE), F32),
            pltpu.VMEM((NEAR, HD, WIDE), F32),
            pltpu.VMEM((NEAR, 8, WIDE), F32),
            pltpu.VMEM((NEAR, 1, WIDE), F32),
            pltpu.VMEM((NEAR, ROWS, WIDE), BF),
        ],
        compiler_params=pltpu.CompilerParams(vmem_limit_bytes=58 * 1024 * 1024),
        cost_estimate=pl.CostEstimate(
            flops=12 * NEAR * WIDE * HD * ROWS * 5, bytes_accessed=10_000_000, transcendentals=10_000_000
        ),
    )(at, lengths, ws, qm, qo, gm, go, kv)


SWAP = [(0, 1), (1, 0)]


def ring(k):
    return [(i, (i + k) % 4) for i in range(4)]


def body(queries, key_rows, value_rows, upstream, loss_weight, doc_lengths):
    x, y, core = lax.axis_index("x"), lax.axis_index("y"), lax.axis_index("core")
    weights_row = loss_weight[0]
    mine_at, other_at = core, 1 - core

    def half(array, at):
        size = array.shape[1] // 2
        return lax.dynamic_slice_in_dim(array, at * size, size, 1)

    kv_mine = jnp.concatenate([half(key_rows[0], mine_at), half(value_rows[0], mine_at)], axis=1)
    kv_send = jnp.concatenate([half(key_rows[0], other_at), half(value_rows[0], other_at)], axis=1)
    kv_other = lax.ppermute(kv_send, "core", SWAP)
    own = jnp.concatenate([kv_mine, kv_other], axis=0)

    r1 = lax.ppermute(own, "x", [(i, i + 1) for i in range(3)])
    r2 = lax.ppermute(own, "x", [(i, i + 2) for i in range(2)])
    three = jnp.concatenate([own, r1, r2], axis=0)
    slots = [None] * SLOTS
    slots[0], slots[4], slots[8] = own, r1, r2
    for k in (1, 3, 2):
        pair = lax.dynamic_slice_in_dim(three, jnp.where(y + k >= 4, ROWS, 0), 2 * ROWS, 0)
        got = lax.ppermute(pair, "y", ring(k))
        slots[k], slots[4 + k] = got[:ROWS], got[ROWS:]
    kv = jnp.stack(slots)

    weighted = (upstream[0].astype(F32) * weights_row[:, None]).astype(BF)
    qm, gm = half(queries[0], mine_at), half(weighted, mine_at)
    qo = lax.ppermute(half(queries[0], other_at), "core", SWAP)
    go = lax.ppermute(half(weighted, other_at), "core", SWAP)

    total = jnp.full((8, 128), jnp.sum(weights_row))
    total = total + lax.ppermute(total, "core", SWAP)
    for axis in ("y", "x", "dp"):
        total = total + sum(lax.ppermute(total, axis, ring(k)) for k in (1, 2, 3))
    at = jnp.stack([4 * x + y, core]).astype(jnp.int32)
    att, dq, dkv = attention(at, doc_lengths[0], total[0, :1], qm, qo, gm, go, kv)

    sums = [dkv[0].astype(F32), dkv[4].astype(F32), dkv[8].astype(F32)]
    for k in (1, 3, 2):
        pair = jnp.concatenate([dkv[k], dkv[4 + k]], axis=0)
        got = lax.ppermute(pair, "y", ring(4 - k)).astype(F32)
        over = y + k >= 4
        first, second = got[:ROWS], got[ROWS:]
        sums[0] = sums[0] + jnp.where(over, 0.0, first)
        sums[1] = sums[1] + jnp.where(over, first, second)
        sums[2] = sums[2] + jnp.where(over, second, 0.0)
    t1 = lax.ppermute(sums[1].astype(BF), "x", [(i + 1, i) for i in range(3)])
    t2 = lax.ppermute(sums[2].astype(BF), "x", [(i + 2, i) for i in range(2)])
    own_grad = (sums[0] + t1.astype(F32) + t2.astype(F32)).astype(BF)

    def join(mine, other):
        got = lax.ppermute(other, "core", SWAP)
        return jnp.where(
            core == 0, jnp.concatenate([mine, got], axis=1), jnp.concatenate([got, mine], axis=1)
        )

    out_rows = join(att[:HALF], att[HALF:])
    dq_rows = join(dq[:HALF], dq[HALF:])
    got = lax.ppermute(own_grad[HALF:], "core", SWAP)
    mine = own_grad[:HALF]
    width = NEAR * HD

    def side(at):
        a, b = mine[:, at:at + width], got[:, at:at + width]
        return jnp.where(core == 0, jnp.concatenate([a, b], axis=1), jnp.concatenate([b, a], axis=1))

    return (out_rows[None], dq_rows[None], side(0)[None], side(width)[None])


def solution(mesh):
    split = Mesh(mesh.devices.reshape(4, 4, 4, 2), ("dp", "x", "y", "core"))
    ctx = ("x", "y", "core")
    rows = P("dp", ctx, None)
    return jax.shard_map(
        body,
        mesh=split,
        in_specs=(rows, rows, rows, rows, P("dp", ctx), P("dp", None)),
        out_specs=(rows, rows, rows, rows),
        check_vma=False,
    )
```

```python
import functools
import math

import jax
import jax.numpy as jnp
from jax import lax
from jax.experimental import pallas as pl
from jax.experimental.pallas import tpu as pltpu
from jax.sharding import Mesh, PartitionSpec as P

QH = 24
KVH = 4
HD = 128
CAP = 30.0
NEAR = 2
GROUP = QH // KVH
ROWS = 256
HALF = 128
WIDE = GROUP * ROWS
TILE = 2 * ROWS
SLOTS = 9
BF = jnp.bfloat16
F32 = jnp.float32
SCALE = HD ** (-0.5)


def dot(a, b, over=(1, 0)):
    return lax.dot_general(a, b, (((over[0],), (over[1],)), ((), ())), preferred_element_type=F32)


def place_x_first(y):
    places = [(0, 0, 0), (1, 0, 4), (2, 0, 8)]
    for at, k in enumerate((1, 3, 2)):
        places += [(3 + at, 0, k), (3 + at, ROWS, 4 + k)]
    return places


def place_y_first(y):
    places = []
    for m in range(3):
        for at, k in enumerate((0, 1, 3, 2)):
            slot = 4 * m + k - jnp.where(y < k, 4, 0)
            places.append((m, at * ROWS, slot))
    return places


def attention_kernel(head, places_of, pieces, at_ref, len_ref, *refs):
    qm_ref, qo_ref, gm_ref, go_ref = refs[:4]
    piece_refs = refs[4:4 + pieces]
    att_ref, dq_ref, dkv_ref = refs[4 + pieces:7 + pieces]
    kv, qs, gs, expo, slope, out_s, dq_s, den, row_dot, ds_buf = refs[7 + pieces:]
    chip = at_ref[0]
    core = at_ref[1]
    row = lax.broadcasted_iota(jnp.int32, (TILE, 1), 0) % ROWS
    row_pos = chip * ROWS + row + jnp.where(row < HALF, core * HALF, (1 - core) * HALF - HALF)
    sub = lax.broadcasted_iota(jnp.int32, (1, ROWS), 1)
    key_off = sub + jnp.where(sub < HALF, core * HALF, (1 - core) * HALF - HALF)

    start = jnp.zeros((TILE, 1), jnp.int32)
    low = jnp.int32(0)
    high = jnp.int32(0)
    edge = jnp.int32(0)
    for j in range(8):
        edge = edge + len_ref[j]
        start = jnp.maximum(start, jnp.where(row_pos >= edge, edge, 0))
        low = jnp.maximum(low, jnp.where(chip * ROWS >= edge, edge, 0))
        high = jnp.maximum(high, jnp.where(chip * ROWS + ROWS - 1 >= edge, edge, 0))

    def needed(slot):
        return (slot <= chip) & ((chip - slot + 1) * ROWS > low)

    for piece, first, slot in places_of(lax.rem(chip, 4)):
        if isinstance(slot, int):
            kv[slot] = piece_refs[piece][first:first + ROWS, :]
        else:
            @pl.when((slot >= 0) & (slot < SLOTS))
            def _():
                kv[jnp.clip(slot, 0, SLOTS - 1)] = piece_refs[piece][first:first + ROWS, :]

    for j in range(GROUP):
        cols = slice((head * GROUP + j) * HD, (head * GROUP + j + 1) * HD)
        for part, (q_in, g_in) in enumerate(((qm_ref, gm_ref), (qo_ref, go_ref))):
            rows = slice(j * ROWS + part * HALF, j * ROWS + (part + 1) * HALF)
            qs[rows, :] = q_in[:, cols]
            gs[rows, :] = g_in[:, cols]
    out_s[...] = jnp.zeros_like(out_s)
    dq_s[...] = jnp.zeros_like(dq_s)
    den[...] = jnp.zeros_like(den)

    def forward(slot, masked):
        keys = kv[slot, :, :HD]
        values = kv[slot, :, HD:]
        for j in range(WIDE // TILE):
            rows = slice(j * TILE, (j + 1) * TILE)
            sq = jnp.tanh(dot(qs[rows, :], keys, (1, 1)) * (SCALE / CAP))
            e = jnp.exp2(sq * (CAP / math.log(2.0)))
            if masked:
                key_pos = (chip - slot) * ROWS + key_off
                e = jnp.where((key_pos >= start) & (key_pos <= row_pos), e, 0.0)
            eb = e.astype(BF)
            expo[slot, rows, :] = eb
            slope[slot, rows, :] = (e * (1.0 - sq * sq)).astype(BF)
            den[rows, :] += e[:, :HD] + e[:, HD:]
            out_s[rows, :] += dot(eb, values)

    def forward_step(slot, carry):
        plain = (slot > 0) & ((chip - slot) * ROWS >= high)

        @pl.when(needed(slot) & plain)
        def _():
            forward(slot, False)

        @pl.when(needed(slot) & jnp.logical_not(plain))
        def _():
            forward(slot, True)

        return carry

    lax.fori_loop(0, SLOTS, forward_step, 0)

    for j in range(GROUP):
        rows = slice(j * ROWS, (j + 1) * ROWS)
        inv = 1.0 / jnp.sum(den[rows, :], axis=1, keepdims=True)
        out = (out_s[rows, :] * inv).astype(BF)
        att_ref[:, j * HD:(j + 1) * HD] = out
        g = (gs[rows, :].astype(F32) * inv).astype(BF)
        gs[rows, :] = g
        row_dot[rows, :] = jnp.broadcast_to(
            jnp.sum(g.astype(F32) * out.astype(F32), axis=1, keepdims=True), (ROWS, HD)
        )

    def backward(slot):
        keys = kv[slot, :, :HD]
        values = kv[slot, :, HD:]
        for j in range(WIDE // TILE):
            rows = slice(j * TILE, (j + 1) * TILE)
            dp = dot(gs[rows, :], values, (1, 1))
            rd = row_dot[rows, :]
            ds = slope[slot, rows, :].astype(F32) * (dp - jnp.concatenate([rd, rd], axis=1))
            ds = ds.astype(BF)
            ds_buf[rows, :] = ds
            dq_s[rows, :] += dot(ds, keys)
        dkv_ref[slot, :, :HD] = (dot(ds_buf[...], qs[...], (0, 0)) * SCALE).astype(BF)
        dkv_ref[slot, :, HD:] = dot(expo[slot], gs[...], (0, 0)).astype(BF)

    def backward_step(slot, carry):
        @pl.when(needed(slot))
        def _():
            backward(slot)

        @pl.when(jnp.logical_not(needed(slot)))
        def _():
            dkv_ref[slot] = jnp.zeros((ROWS, 2 * HD), BF)

        return carry

    lax.fori_loop(0, SLOTS, backward_step, 0)

    for j in range(GROUP):
        rows = slice(j * ROWS, (j + 1) * ROWS)
        dq_ref[:, j * HD:(j + 1) * HD] = (dq_s[rows, :] * SCALE).astype(BF)


def attention(head, places_of, at, lengths, qm, qo, gm, go, *pieces):
    smem = pl.BlockSpec(memory_space=pltpu.SMEM)
    vmem = pl.BlockSpec(memory_space=pltpu.VMEM)
    return pl.pallas_call(
        functools.partial(attention_kernel, head, places_of, len(pieces)),
        out_shape=(
            jax.ShapeDtypeStruct((ROWS, GROUP * HD), BF),
            jax.ShapeDtypeStruct((ROWS, GROUP * HD), BF),
            jax.ShapeDtypeStruct((SLOTS, ROWS, 2 * HD), BF),
        ),
        in_specs=[smem] * 2 + [vmem] * (4 + len(pieces)),
        out_specs=(vmem,) * 3,
        scratch_shapes=[
            pltpu.VMEM((SLOTS, ROWS, 2 * HD), BF),
            pltpu.VMEM((WIDE, HD), BF),
            pltpu.VMEM((WIDE, HD), BF),
            pltpu.VMEM((SLOTS, WIDE, ROWS), BF),
            pltpu.VMEM((SLOTS, WIDE, ROWS), BF),
            pltpu.VMEM((WIDE, HD), F32),
            pltpu.VMEM((WIDE, HD), F32),
            pltpu.VMEM((WIDE, HD), F32),
            pltpu.VMEM((WIDE, HD), F32),
            pltpu.VMEM((WIDE, ROWS), BF),
        ],
        compiler_params=pltpu.CompilerParams(vmem_limit_bytes=40 * 1024 * 1024),
        cost_estimate=pl.CostEstimate(
            flops=12 * WIDE * HD * ROWS * SLOTS * 4, bytes_accessed=6_000_000, transcendentals=7_000_000
        ),
    )(at, lengths, qm, qo, gm, go, *pieces)


SWAP = [(0, 1), (1, 0)]


def ring(k):
    return [(i, (i + k) % 4) for i in range(4)]


def gather_x_first(own, y):
    r1 = lax.ppermute(own, "x", ring(1))
    r2 = lax.ppermute(own, "x", ring(2))
    three = jnp.concatenate([own, r1, r2], axis=0)
    pieces = [own, r1, r2]
    for k in (1, 3, 2):
        pair = lax.dynamic_slice_in_dim(three, jnp.where(y + k >= 4, ROWS, 0), 2 * ROWS, 0)
        pieces.append(lax.ppermute(pair, "y", ring(k)))
    return pieces


def gather_y_first(own):
    near = jnp.concatenate([own] + [lax.ppermute(own, "y", ring(k)) for k in (1, 3, 2)], axis=0)
    return [near, lax.ppermute(near, "x", ring(1)), lax.ppermute(near, "x", ring(2))]


def after(value, token):
    return lax.optimization_barrier((value, token))[0]


def send_y(dkv):
    return [
        lax.ppermute(jnp.concatenate([dkv[k], dkv[4 + k]], axis=0), "y", ring(4 - k)) for k in (1, 3, 2)
    ]


def scatter_y(dkv, received, y):
    sums = [dkv[0].astype(F32), dkv[4].astype(F32), dkv[8].astype(F32)]
    for k, got in zip((1, 3, 2), received):
        got = got.astype(F32)
        over = y + k >= 4
        first, second = got[:ROWS], got[ROWS:]
        sums[0] = sums[0] + jnp.where(over, 0.0, first)
        sums[1] = sums[1] + jnp.where(over, first, second)
        sums[2] = sums[2] + jnp.where(over, second, 0.0)
    return sums[0], sums[1].astype(BF), sums[2].astype(BF)


def scatter_x(sums):
    t1 = lax.ppermute(sums[1], "x", ring(3))
    t2 = lax.ppermute(sums[2], "x", ring(2))
    return sums[0] + t1.astype(F32) + t2.astype(F32)


def body(queries, key_rows, value_rows, upstream, loss_weight, doc_lengths):
    x, y, core = lax.axis_index("x"), lax.axis_index("y"), lax.axis_index("core")
    weights_row = loss_weight[0]
    mine_at, other_at = core, 1 - core

    def half(array, at):
        size = array.shape[1] // 2
        return lax.dynamic_slice_in_dim(array, at * size, size, 1)

    def heads(at):
        k, v = half(key_rows[0], at), half(value_rows[0], at)
        return jnp.concatenate([k[:, :HD], v[:, :HD], k[:, HD:], v[:, HD:]], axis=1)

    kv_other = lax.ppermute(heads(other_at), "core", SWAP)
    own = jnp.concatenate([heads(mine_at), kv_other], axis=0)
    first, second = own[:, :2 * HD], own[:, 2 * HD:]
    first_pieces = gather_x_first(first, y)
    second_pieces = gather_y_first(second)

    weighted = (upstream[0].astype(F32) * weights_row[:, None]).astype(BF)
    qm, gm = half(queries[0], mine_at), half(weighted, mine_at)
    qo = lax.ppermute(half(queries[0], other_at), "core", SWAP)
    go = lax.ppermute(half(weighted, other_at), "core", SWAP)

    at = jnp.stack([4 * x + y, core]).astype(jnp.int32)
    lengths = doc_lengths[0]
    att0, dq0, dkv0 = attention(0, place_x_first, at, lengths, qm, qo, gm, go, *first_pieces)
    att1, dq1, dkv1 = attention(1, place_y_first, at, lengths, qm, qo, gm, go, *second_pieces)

    sent0 = send_y(dkv0)
    sent0 = after(sent0, dkv1)
    sent1 = send_y(dkv1)
    sums0 = scatter_y(dkv0, sent0, y)

    total = jnp.full((8, 128), jnp.sum(weights_row))
    total = total + lax.ppermute(total, "core", SWAP)
    for axis, token in (("y", second_pieces[0]), ("x", att0), ("dp", att1)):
        total = after(total, token)
        total = total + sum(lax.ppermute(total, axis, ring(k)) for k in (1, 2, 3))
    inv = 1.0 / total[0, 0]

    grad0 = scatter_x(sums0)
    grad1 = scatter_x(scatter_y(dkv1, sent1, y))
    own_grad = jnp.concatenate([grad0, grad1], axis=1).astype(BF)

    def join(a, b, scale):
        got_a = lax.ppermute(a[HALF:], "core", SWAP)
        got_b = lax.ppermute(b[HALF:], "core", SWAP)
        a, b = a[:HALF], b[:HALF]
        low = jnp.concatenate([a, b, got_a, got_b], axis=1)
        high = jnp.concatenate([got_a, got_b, a, b], axis=1)
        both = jnp.where(core == 0, low, high)
        return both if scale is None else (both.astype(F32) * scale).astype(BF)

    out_rows = join(att0, att1, None)
    dq_rows = join(dq0, dq1, inv)
    got = lax.ppermute(own_grad[HALF:], "core", SWAP)
    mine = own_grad[:HALF]

    def side(at):
        a = [mine[:, at:at + HD], mine[:, at + 2 * HD:at + 3 * HD]]
        b = [got[:, at:at + HD], got[:, at + 2 * HD:at + 3 * HD]]
        both = jnp.where(core == 0, jnp.concatenate(a + b, axis=1), jnp.concatenate(b + a, axis=1))
        return (both.astype(F32) * inv).astype(BF)

    return (out_rows[None], dq_rows[None], side(0)[None], side(HD)[None])


def solution(mesh):
    split = Mesh(mesh.devices.reshape(4, 4, 4, 2), ("dp", "x", "y", "core"))
    ctx = ("x", "y", "core")
    rows = P("dp", ctx, None)
    return jax.shard_map(
        body,
        mesh=split,
        in_specs=(rows, rows, rows, rows, P("dp", ctx), P("dp", None)),
        out_specs=(rows, rows, rows, rows),
        check_vma=False,
    )
```

```python
import functools
import math

import jax
import jax.numpy as jnp
from jax import lax
from jax.experimental import pallas as pl
from jax.experimental.pallas import tpu as pltpu
from jax.sharding import Mesh, PartitionSpec as P

QH = 24
KVH = 4
HD = 128
CAP = 30.0
NEAR = 2
GROUP = QH // KVH
ROWS = 256
HALF = 128
WIDE = GROUP * ROWS
TILE = 2 * ROWS
NOTE = 16
SLOTS = 9
BF = jnp.bfloat16
F32 = jnp.float32
SCALE = HD ** (-0.5)


def dot(a, b, over=(1, 0)):
    return lax.dot_general(a, b, (((over[0],), (over[1],)), ((), ())), preferred_element_type=F32)


def place_x_first(y):
    places = [(0, 0, 0), (1, 0, 4), (2, 0, 8)]
    for at, k in enumerate((1, 3, 2)):
        places += [(3 + at, 0, k), (3 + at, ROWS, 4 + k)]
    return places


def place_y_first(y):
    places = []
    for m in range(3):
        for at, k in enumerate((0, 1, 3, 2)):
            slot = 4 * m + k - jnp.where(y < k, 4, 0)
            places.append((m, at * (ROWS + NOTE), slot))
    return places


def attention_kernel(head, places_of, pieces, at_ref, len_ref, *refs):
    qm_ref, qo_ref, gm_ref, go_ref = refs[:4]
    piece_refs = refs[4:4 + pieces]
    att_ref, dq_ref, dkv_ref = refs[4 + pieces:7 + pieces]
    kv, qs, gs, expo, slope, out_s, dq_s, den, row_dot, ds_buf = refs[7 + pieces:]
    chip = at_ref[0]
    core = at_ref[1]
    row = lax.broadcasted_iota(jnp.int32, (TILE, 1), 0) % ROWS
    row_pos = chip * ROWS + row + jnp.where(row < HALF, core * HALF, (1 - core) * HALF - HALF)
    sub = lax.broadcasted_iota(jnp.int32, (1, ROWS), 1)
    key_off = sub + jnp.where(sub < HALF, core * HALF, (1 - core) * HALF - HALF)

    start = jnp.zeros((TILE, 1), jnp.int32)
    low = jnp.int32(0)
    high = jnp.int32(0)
    edge = jnp.int32(0)
    for j in range(8):
        edge = edge + len_ref[j]
        start = jnp.maximum(start, jnp.where(row_pos >= edge, edge, 0))
        low = jnp.maximum(low, jnp.where(chip * ROWS >= edge, edge, 0))
        high = jnp.maximum(high, jnp.where(chip * ROWS + ROWS - 1 >= edge, edge, 0))

    def needed(slot):
        return (slot <= chip) & ((chip - slot + 1) * ROWS > low)

    for piece, first, slot in places_of(lax.rem(chip, 4)):
        if isinstance(slot, int):
            kv[slot] = piece_refs[piece][first:first + ROWS, :]
        else:
            @pl.when((slot >= 0) & (slot < SLOTS))
            def _():
                kv[jnp.clip(slot, 0, SLOTS - 1)] = piece_refs[piece][first:first + ROWS, :]

    for j in range(GROUP):
        cols = slice((head * GROUP + j) * HD, (head * GROUP + j + 1) * HD)
        for part, (q_in, g_in) in enumerate(((qm_ref, gm_ref), (qo_ref, go_ref))):
            rows = slice(j * ROWS + part * HALF, j * ROWS + (part + 1) * HALF)
            qs[rows, :] = q_in[:, cols]
            gs[rows, :] = g_in[:, cols]
    out_s[...] = jnp.zeros_like(out_s)
    dq_s[...] = jnp.zeros_like(dq_s)
    den[...] = jnp.zeros_like(den)

    def forward(slot, masked):
        keys = kv[slot, :, :HD]
        values = kv[slot, :, HD:]
        for j in range(WIDE // TILE):
            rows = slice(j * TILE, (j + 1) * TILE)
            sq = jnp.tanh(dot(qs[rows, :], keys, (1, 1)) * (SCALE / CAP))
            e = jnp.exp2(sq * (CAP / math.log(2.0)))
            if masked:
                key_pos = (chip - slot) * ROWS + key_off
                e = jnp.where((key_pos >= start) & (key_pos <= row_pos), e, 0.0)
            eb = e.astype(BF)
            expo[slot, rows, :] = eb
            slope[slot, rows, :] = (e * (1.0 - sq * sq)).astype(BF)
            den[rows, :] += e[:, :HD] + e[:, HD:]
            out_s[rows, :] += dot(eb, values)

    def forward_step(slot, carry):
        plain = (slot > 0) & ((chip - slot) * ROWS >= high)

        @pl.when(needed(slot) & plain)
        def _():
            forward(slot, False)

        @pl.when(needed(slot) & jnp.logical_not(plain))
        def _():
            forward(slot, True)

        return carry

    lax.fori_loop(0, SLOTS, forward_step, 0)

    for j in range(GROUP):
        rows = slice(j * ROWS, (j + 1) * ROWS)
        inv = 1.0 / jnp.sum(den[rows, :], axis=1, keepdims=True)
        out = (out_s[rows, :] * inv).astype(BF)
        att_ref[:, j * HD:(j + 1) * HD] = out
        g = (gs[rows, :].astype(F32) * inv).astype(BF)
        gs[rows, :] = g
        row_dot[rows, :] = jnp.broadcast_to(
            jnp.sum(g.astype(F32) * out.astype(F32), axis=1, keepdims=True), (ROWS, HD)
        )

    def backward(slot):
        keys = kv[slot, :, :HD]
        values = kv[slot, :, HD:]
        for j in range(WIDE // TILE):
            rows = slice(j * TILE, (j + 1) * TILE)
            dp = dot(gs[rows, :], values, (1, 1))
            rd = row_dot[rows, :]
            ds = slope[slot, rows, :].astype(F32) * (dp - jnp.concatenate([rd, rd], axis=1))
            ds = ds.astype(BF)
            ds_buf[rows, :] = ds
            dq_s[rows, :] += dot(ds, keys)
        dkv_ref[slot, :, :HD] = (dot(ds_buf[...], qs[...], (0, 0)) * SCALE).astype(BF)
        dkv_ref[slot, :, HD:] = dot(expo[slot], gs[...], (0, 0)).astype(BF)

    def backward_step(slot, carry):
        @pl.when(needed(slot))
        def _():
            backward(slot)

        @pl.when(jnp.logical_not(needed(slot)))
        def _():
            dkv_ref[slot] = jnp.zeros((ROWS, 2 * HD), BF)

        return carry

    lax.fori_loop(0, SLOTS, backward_step, 0)

    for j in range(GROUP):
        rows = slice(j * ROWS, (j + 1) * ROWS)
        dq_ref[:, j * HD:(j + 1) * HD] = (dq_s[rows, :] * SCALE).astype(BF)


def attention(head, places_of, at, lengths, qm, qo, gm, go, *pieces):
    smem = pl.BlockSpec(memory_space=pltpu.SMEM)
    vmem = pl.BlockSpec(memory_space=pltpu.VMEM)
    return pl.pallas_call(
        functools.partial(attention_kernel, head, places_of, len(pieces)),
        out_shape=(
            jax.ShapeDtypeStruct((ROWS, GROUP * HD), BF),
            jax.ShapeDtypeStruct((ROWS, GROUP * HD), BF),
            jax.ShapeDtypeStruct((SLOTS, ROWS, 2 * HD), BF),
        ),
        in_specs=[smem] * 2 + [vmem] * (4 + len(pieces)),
        out_specs=(vmem,) * 3,
        scratch_shapes=[
            pltpu.VMEM((SLOTS, ROWS, 2 * HD), BF),
            pltpu.VMEM((WIDE, HD), BF),
            pltpu.VMEM((WIDE, HD), BF),
            pltpu.VMEM((SLOTS, WIDE, ROWS), BF),
            pltpu.VMEM((SLOTS, WIDE, ROWS), BF),
            pltpu.VMEM((WIDE, HD), F32),
            pltpu.VMEM((WIDE, HD), F32),
            pltpu.VMEM((WIDE, HD), F32),
            pltpu.VMEM((WIDE, HD), F32),
            pltpu.VMEM((WIDE, ROWS), BF),
        ],
        compiler_params=pltpu.CompilerParams(vmem_limit_bytes=40 * 1024 * 1024),
        cost_estimate=pl.CostEstimate(
            flops=12 * WIDE * HD * ROWS * SLOTS * 4, bytes_accessed=6_000_000, transcendentals=7_000_000
        ),
    )(at, lengths, qm, qo, gm, go, *pieces)


SWAP = [(0, 1), (1, 0)]


def ring(k):
    return [(i, (i + k) % 4) for i in range(4)]


def note(value, width):
    high = lax.reduce_precision(value, 8, 7)
    middle = lax.reduce_precision(value - high, 8, 7)
    column = lax.broadcasted_iota(jnp.int32, (NOTE, width), 1)
    rest = value - high - middle
    parts = jnp.where(column == 0, high, jnp.where(column == 1, middle, jnp.where(column == 2, rest, 0.0)))
    return parts.astype(BF)


def noted(array, row):
    return jnp.sum(array[row, :3].astype(F32))


def after(value, token):
    return lax.optimization_barrier((value, token))[0]


def send_y(dkv):
    return [
        lax.ppermute(jnp.concatenate([dkv[k], dkv[4 + k]], axis=0), "y", ring(4 - k)) for k in (1, 3, 2)
    ]


def scatter_y(dkv, received, y):
    sums = [dkv[0].astype(F32), dkv[4].astype(F32), dkv[8].astype(F32)]
    for k, got in zip((1, 3, 2), received):
        got = got.astype(F32)
        over = y + k >= 4
        first, second = got[:ROWS], got[ROWS:]
        sums[0] = sums[0] + jnp.where(over, 0.0, first)
        sums[1] = sums[1] + jnp.where(over, first, second)
        sums[2] = sums[2] + jnp.where(over, second, 0.0)
    return sums[0], sums[1].astype(BF), sums[2].astype(BF)


def scatter_x(sums):
    t1 = lax.ppermute(sums[1], "x", ring(3))
    t2 = lax.ppermute(sums[2], "x", ring(2))
    return sums[0] + t1.astype(F32) + t2.astype(F32)


def body(queries, key_rows, value_rows, upstream, loss_weight, doc_lengths):
    x, y, core = lax.axis_index("x"), lax.axis_index("y"), lax.axis_index("core")
    weights_row = loss_weight[0]
    mine_at, other_at = core, 1 - core

    def half(array, at):
        size = array.shape[1] // 2
        return lax.dynamic_slice_in_dim(array, at * size, size, 1)

    def heads(at):
        k, v = half(key_rows[0], at), half(value_rows[0], at)
        return jnp.concatenate([k[:, :HD], v[:, :HD], k[:, HD:], v[:, HD:]], axis=1)

    part = jnp.sum(weights_row)
    kv_other = lax.ppermute(jnp.concatenate([heads(other_at), note(part, 4 * HD)], axis=0), "core", SWAP)
    chip_total = part + noted(kv_other, HALF)
    own = jnp.concatenate([heads(mine_at), kv_other[:HALF]], axis=0)
    first = own[:, :2 * HD]
    second = jnp.concatenate([own[:, 2 * HD:], note(chip_total, 2 * HD)], axis=0)
    r1 = lax.ppermute(first, "x", ring(1))
    r2 = lax.ppermute(first, "x", ring(2))
    near = jnp.concatenate([second] + [lax.ppermute(second, "y", ring(k)) for k in (1, 3, 2)], axis=0)

    weighted = (upstream[0].astype(F32) * weights_row[:, None]).astype(BF)
    qm, gm = half(queries[0], mine_at), half(weighted, mine_at)
    q_send, g_send = after((half(queries[0], other_at), half(weighted, other_at)), first)
    qo = lax.ppermute(q_send, "core", SWAP)
    go = lax.ppermute(g_send, "core", SWAP)

    three = jnp.concatenate([first, r1, r2], axis=0)
    three, near = after((three, near), (qo, go))
    first_pieces = [first, r1, r2]
    for k in (1, 3, 2):
        pair = lax.dynamic_slice_in_dim(three, jnp.where(y + k >= 4, ROWS, 0), 2 * ROWS, 0)
        first_pieces.append(lax.ppermute(pair, "y", ring(k)))
    second_pieces = [near, lax.ppermute(near, "x", ring(1)), lax.ppermute(near, "x", ring(2))]

    at = jnp.stack([4 * x + y, core]).astype(jnp.int32)
    lengths = doc_lengths[0]
    att0, dq0, dkv0 = attention(0, place_x_first, at, lengths, qm, qo, gm, go, *first_pieces)
    att1, dq1, dkv1 = attention(1, place_y_first, after(at, att0), lengths, qm, qo, gm, go, *second_pieces)

    sent0 = send_y(dkv0)
    sums0 = scatter_y(dkv0, after(sent0, dkv1), y)
    sent1 = send_y(after(dkv1, sums0))
    sums1 = scatter_y(dkv1, sent1, y)
    grad0 = scatter_x(after(sums0, sent1[0]))
    grad1 = scatter_x(sums1)

    rows_total = sum(noted(near, at * (ROWS + NOTE) + ROWS) for at in range(4))
    total = jnp.full((8, 128), after(rows_total, att0))
    total = total + lax.ppermute(total, "x", ring(3))
    for piece in second_pieces[1:]:
        total = total + sum(noted(piece, at * (ROWS + NOTE) + ROWS) for at in range(4))
    total = after(total, grad0)
    total = total + sum(lax.ppermute(total, "dp", ring(k)) for k in (1, 2, 3))
    inv = 1.0 / total[0, 0]

    own_grad = jnp.concatenate([grad0, grad1], axis=1).astype(BF)

    width = GROUP * HD
    parts = [att0, att1, dq0, dq1]
    others = jnp.concatenate([part[HALF:] for part in parts], axis=1)
    others = lax.ppermute(after(others, sums1[1]), "core", SWAP)

    def join(at):
        ours = jnp.concatenate([parts[at][:HALF], parts[at + 1][:HALF]], axis=1)
        theirs = others[:, at * width:(at + 2) * width]
        low = jnp.concatenate([ours, theirs], axis=1)
        high = jnp.concatenate([theirs, ours], axis=1)
        return jnp.where(core == 0, low, high)

    out_rows = join(0)
    dq_rows = (join(2).astype(F32) * inv).astype(BF)
    got = lax.ppermute(own_grad[HALF:], "core", SWAP)
    mine = own_grad[:HALF]

    def side(at):
        a = [mine[:, at:at + HD], mine[:, at + 2 * HD:at + 3 * HD]]
        b = [got[:, at:at + HD], got[:, at + 2 * HD:at + 3 * HD]]
        both = jnp.where(core == 0, jnp.concatenate(a + b, axis=1), jnp.concatenate(b + a, axis=1))
        return (both.astype(F32) * inv).astype(BF)

    return (out_rows[None], dq_rows[None], side(0)[None], side(HD)[None])


def solution(mesh):
    split = Mesh(mesh.devices.reshape(4, 4, 4, 2), ("dp", "x", "y", "core"))
    ctx = ("x", "y", "core")
    rows = P("dp", ctx, None)
    return jax.shard_map(
        body,
        mesh=split,
        in_specs=(rows, rows, rows, rows, P("dp", ctx), P("dp", None)),
        out_specs=(rows, rows, rows, rows),
        check_vma=False,
    )
```

```python
import functools
import math

import jax
import jax.numpy as jnp
from jax import lax
from jax.experimental import pallas as pl
from jax.experimental.pallas import tpu as pltpu
from jax.sharding import Mesh, PartitionSpec as P

QH = 24
KVH = 4
HD = 128
CAP = 30.0
NEAR = 2
GROUP = QH // KVH
ROWS = 256
HALF = 128
WIDE = GROUP * ROWS
TILE = HALF
NOTE = 16
SLOTS = 9
BF = jnp.bfloat16
F32 = jnp.float32
SCALE = HD ** (-0.5)


def dot(a, b, over=(1, 0)):
    return lax.dot_general(a, b, (((over[0],), (over[1],)), ((), ())), preferred_element_type=F32)


def place_x_first(y):
    places = [(0, 0, 0), (1, 0, 4), (2, 0, 8)]
    for at, k in enumerate((1, 3, 2)):
        places += [(3 + at, 0, k), (3 + at, ROWS, 4 + k)]
    return places


def place_y_first(y):
    places = []
    for m in range(3):
        for at, k in enumerate((0, 1, 3, 2)):
            slot = 4 * m + k - jnp.where(y < k, 4, 0)
            places.append((m, at * (ROWS + NOTE), slot))
    return places


def attention_kernel(head, places_of, pieces, at_ref, len_ref, *refs):
    qm_ref, qo_ref, gm_ref, go_ref = refs[:4]
    piece_refs = refs[4:4 + pieces]
    att_ref, dq_ref, self_ref, *pair_refs = refs[4 + pieces:10 + pieces]
    keys, values, qs, gs, expo, slope, row_dot, dkv = refs[10 + pieces:]
    chip = at_ref[0]
    core = at_ref[1]
    row = lax.broadcasted_iota(jnp.int32, (HALF, 1), 0) + chip * ROWS
    row_pos = [row + core * HALF, row + (1 - core) * HALF]
    sub = lax.broadcasted_iota(jnp.int32, (1, ROWS), 1)
    key_off = sub + jnp.where(sub < HALF, core * HALF, (1 - core) * HALF - HALF)

    start = [jnp.zeros((HALF, 1), jnp.int32)] * 2
    low = jnp.int32(0)
    high = jnp.int32(0)
    edge = jnp.int32(0)
    for j in range(8):
        edge = edge + len_ref[j]
        start = [jnp.maximum(s, jnp.where(p >= edge, edge, 0)) for s, p in zip(start, row_pos)]
        low = jnp.maximum(low, jnp.where(chip * ROWS >= edge, edge, 0))
        high = jnp.maximum(high, jnp.where(chip * ROWS + ROWS - 1 >= edge, edge, 0))

    def needed(slot):
        return (slot <= chip) & ((chip - slot + 1) * ROWS > low)

    def block(slot):
        return pl.ds(pl.multiple_of(slot * ROWS, ROWS), ROWS)

    values[:, HD:] = jnp.ones((SLOTS * ROWS, HD), BF)
    for piece, first, slot in places_of(lax.rem(chip, 4)):
        @pl.when((slot >= 0) & (slot < SLOTS))
        def _():
            to = block(jnp.clip(slot, 0, SLOTS - 1))
            keys[to, :] = piece_refs[piece][first:first + ROWS, :HD]
            values[to, :HD] = piece_refs[piece][first:first + ROWS, HD:]

    for j in range(GROUP):
        cols = slice((head * GROUP + j) * HD, (head * GROUP + j + 1) * HD)
        for part, (q_in, g_in) in enumerate(((qm_ref, gm_ref), (qo_ref, go_ref))):
            rows = slice(j * ROWS + part * HALF, j * ROWS + (part + 1) * HALF)
            qs[rows, :] = q_in[:, cols]
            gs[rows, :] = g_in[:, cols]

    def forward(slot, masked):
        block_keys = keys[block(slot), :]
        for j in range(WIDE // TILE):
            rows = slice(j * TILE, (j + 1) * TILE)
            sq = jnp.tanh(dot(qs[rows, :], block_keys, (1, 1)) * (SCALE / CAP))
            e = jnp.exp2(sq * (CAP / math.log(2.0)))
            if masked:
                key_pos = (chip - slot) * ROWS + key_off
                e = jnp.where((key_pos >= start[j % 2]) & (key_pos <= row_pos[j % 2]), e, 0.0)
            expo[rows, block(slot)] = e.astype(BF)
            slope[rows, block(slot)] = (e * (1.0 - sq * sq)).astype(BF)

    def forward_step(slot, carry):
        plain = (slot > 0) & ((chip - slot) * ROWS >= high)

        @pl.when(needed(slot) & plain)
        def _():
            forward(slot, False)

        @pl.when(needed(slot) & jnp.logical_not(plain))
        def _():
            forward(slot, True)

        @pl.when(jnp.logical_not(needed(slot)))
        def _():
            expo[:, block(slot)] = jnp.zeros((WIDE, ROWS), BF)
            slope[:, block(slot)] = jnp.zeros((WIDE, ROWS), BF)

        return carry

    lax.fori_loop(0, SLOTS, forward_step, 0)

    for j in range(GROUP):
        rows = slice(j * ROWS, (j + 1) * ROWS)
        mixed = dot(expo[rows, :], values[...])
        inv = 1.0 / mixed[:, HD:]
        out = (mixed[:, :HD] * inv).astype(BF)
        att_ref[:, j * HD:(j + 1) * HD] = out
        g = (gs[rows, :].astype(F32) * inv).astype(BF)
        gs[rows, :] = g
        row_dot[rows, :] = jnp.broadcast_to(
            jnp.sum(g.astype(F32) * out.astype(F32), axis=1, keepdims=True), (ROWS, HD)
        )

    def backward(slot):
        block_values = values[block(slot), :HD]
        for j in range(WIDE // TILE):
            rows = slice(j * TILE, (j + 1) * TILE)
            dp = dot(gs[rows, :], block_values, (1, 1))
            rd = row_dot[rows, :]
            ds = slope[rows, block(slot)].astype(F32) * (dp - jnp.concatenate([rd, rd], axis=1))
            slope[rows, block(slot)] = ds.astype(BF)
        dkv[slot, :, :HD] = (dot(slope[:, block(slot)], qs[...], (0, 0)) * SCALE).astype(BF)
        dkv[slot, :, HD:] = dot(expo[:, block(slot)], gs[...], (0, 0)).astype(BF)

    def backward_step(slot, carry):
        @pl.when(needed(slot))
        def _():
            backward(slot)

        @pl.when(jnp.logical_not(needed(slot)))
        def _():
            dkv[slot] = jnp.zeros((ROWS, 2 * HD), BF)

        return carry

    lax.fori_loop(0, SLOTS, backward_step, 0)

    for j in range(GROUP):
        rows = slice(j * ROWS, (j + 1) * ROWS)
        dq_ref[:, j * HD:(j + 1) * HD] = (dot(slope[rows, :], keys[...]) * SCALE).astype(BF)
    for m in range(3):
        self_ref[m] = dkv[4 * m]
    for pair_ref, k in zip(pair_refs, (1, 3, 2)):
        pair_ref[:ROWS, :] = dkv[k]
        pair_ref[ROWS:, :] = dkv[4 + k]


def attention(head, places_of, at, lengths, qm, qo, gm, go, *pieces):
    smem = pl.BlockSpec(memory_space=pltpu.SMEM)
    vmem = pl.BlockSpec(memory_space=pltpu.VMEM)
    return pl.pallas_call(
        functools.partial(attention_kernel, head, places_of, len(pieces)),
        out_shape=(
            jax.ShapeDtypeStruct((ROWS, GROUP * HD), BF),
            jax.ShapeDtypeStruct((ROWS, GROUP * HD), BF),
            jax.ShapeDtypeStruct((3, ROWS, 2 * HD), BF),
        ) + (jax.ShapeDtypeStruct((2 * ROWS, 2 * HD), BF),) * 3,
        in_specs=[smem] * 2 + [vmem] * (4 + len(pieces)),
        out_specs=(vmem,) * 6,
        scratch_shapes=[
            pltpu.VMEM((SLOTS * ROWS, HD), BF),
            pltpu.VMEM((SLOTS * ROWS, 2 * HD), BF),
            pltpu.VMEM((WIDE, HD), BF),
            pltpu.VMEM((WIDE, HD), BF),
            pltpu.VMEM((WIDE, SLOTS * ROWS), BF),
            pltpu.VMEM((WIDE, SLOTS * ROWS), BF),
            pltpu.VMEM((WIDE, HD), F32),
            pltpu.VMEM((SLOTS, ROWS, 2 * HD), BF),
        ],
        compiler_params=pltpu.CompilerParams(vmem_limit_bytes=40 * 1024 * 1024),
        cost_estimate=pl.CostEstimate(
            flops=12 * WIDE * HD * ROWS * SLOTS * 4, bytes_accessed=6_000_000, transcendentals=7_000_000
        ),
    )(at, lengths, qm, qo, gm, go, *pieces)


def inverse(total_ref):
    total = jnp.sum(total_ref[...], axis=0, keepdims=True)
    return 1.0 / jnp.sum(total, axis=1, keepdims=True)


def finish_rows(core_ref, total_ref, att0, att1, dq0, dq1, others, out_ref, dq_ref):
    inv = inverse(total_ref)
    width = GROUP * HD
    for at, pair in ((0, (att0, att1)), (2, (dq0, dq1))):
        for to, mine in ((0, core_ref[0] == 0), (2 * width, core_ref[0] != 0)):
            for j, part in enumerate(pair):
                theirs = others[:, (at + j) * width:(at + j + 1) * width]
                rows = jnp.where(mine, part[:HALF, :], theirs)
                cols = slice(to + j * width, to + (j + 1) * width)
                if at == 0:
                    out_ref[:, cols] = rows
                else:
                    dq_ref[:, cols] = (rows.astype(F32) * inv).astype(BF)


def finish_keys(core_ref, total_ref, own, got, key_ref, value_ref):
    inv = inverse(total_ref)
    for to, mine in ((0, core_ref[0] == 0), (NEAR * HD, core_ref[0] != 0)):
        for h in range(NEAR):
            cols = slice(to + h * HD, to + (h + 1) * HD)
            for at, ref in ((2 * h * HD, key_ref), ((2 * h + 1) * HD, value_ref)):
                rows = jnp.where(mine, own[:HALF, at:at + HD], got[:, at:at + HD])
                ref[:, cols] = (rows.astype(F32) * inv).astype(BF)


def finish(kernel, core, *arrays, outs, width):
    vmem = pl.BlockSpec(memory_space=pltpu.VMEM)
    return pl.pallas_call(
        kernel,
        out_shape=(jax.ShapeDtypeStruct((HALF, width), BF),) * outs,
        in_specs=[pl.BlockSpec(memory_space=pltpu.SMEM)] + [vmem] * len(arrays),
        out_specs=(vmem,) * outs,
        compiler_params=pltpu.CompilerParams(vmem_limit_bytes=16 * 1024 * 1024),
    )(core.astype(jnp.int32).reshape(1), *arrays)


SWAP = [(0, 1), (1, 0)]


def ring(k):
    return [(i, (i + k) % 4) for i in range(4)]


def note(values):
    high = lax.reduce_precision(values, 8, 7)
    middle = lax.reduce_precision(values - high, 8, 7)
    rest = values - high - middle
    row = lax.broadcasted_iota(jnp.int32, (NOTE, HD), 0)
    parts = jnp.where(row == 0, high, jnp.where(row == 1, middle, jnp.where(row == 2, rest, 0.0)))
    return jnp.concatenate([parts, parts], axis=1).astype(BF)


def noted(array):
    return sum(array[at + ROWS:at + ROWS + 3, :HD].astype(F32) for at in range(0, 4 * (ROWS + NOTE), ROWS + NOTE))


def after(value, token):
    return lax.optimization_barrier((value, token))[0]


def send_y(pairs):
    return [lax.ppermute(pair, "y", ring(4 - k)) for pair, k in zip(pairs, (1, 3, 2))]


def scatter_y(selves, received, y):
    sums = [selves[m].astype(F32) for m in range(3)]
    for k, got in zip((1, 3, 2), received):
        got = got.astype(F32)
        over = y + k >= 4
        first, second = got[:ROWS], got[ROWS:]
        sums[0] = sums[0] + jnp.where(over, 0.0, first)
        sums[1] = sums[1] + jnp.where(over, first, second)
        sums[2] = sums[2] + jnp.where(over, second, 0.0)
    return sums[0], sums[1].astype(BF), sums[2].astype(BF)


def scatter_x(sums):
    t1 = lax.ppermute(sums[1], "x", ring(3))
    t2 = lax.ppermute(sums[2], "x", ring(2))
    return sums[0] + t1.astype(F32) + t2.astype(F32)


def body(queries, key_rows, value_rows, upstream, loss_weight, doc_lengths):
    x, y, core = lax.axis_index("x"), lax.axis_index("y"), lax.axis_index("core")
    weights_row = loss_weight[0]
    mine_at, other_at = core, 1 - core

    def half(array, at):
        size = array.shape[1] // 2
        return lax.dynamic_slice_in_dim(array, at * size, size, 1)

    def heads(at):
        k, v = half(key_rows[0], at), half(value_rows[0], at)
        return jnp.concatenate([k[:, :HD], v[:, :HD], k[:, HD:], v[:, HD:]], axis=1)

    weights = jnp.broadcast_to(weights_row[None], (8, HD))
    weights = weights + lax.ppermute(weights, "core", SWAP)
    kv_other = lax.ppermute(heads(other_at), "core", SWAP)
    own = jnp.concatenate([heads(mine_at), kv_other], axis=0)
    first = own[:, :2 * HD]
    second = jnp.concatenate([own[:, 2 * HD:], note(weights[:1])], axis=0)
    r1 = lax.ppermute(first, "x", ring(1))
    r2 = lax.ppermute(first, "x", ring(2))
    near = jnp.concatenate([second] + [lax.ppermute(second, "y", ring(k)) for k in (1, 3, 2)], axis=0)

    weighted = (upstream[0].astype(F32) * weights_row[:, None]).astype(BF)
    qm, gm = half(queries[0], mine_at), half(weighted, mine_at)
    q_send, g_send = after((half(queries[0], other_at), half(weighted, other_at)), first)
    qo = lax.ppermute(q_send, "core", SWAP)
    go = lax.ppermute(g_send, "core", SWAP)

    three = jnp.concatenate([first, r1, r2], axis=0)
    three = after(three, (qo, go))
    first_pieces = [first, r1, r2]
    for k in (1, 3, 2):
        pair = lax.dynamic_slice_in_dim(three, jnp.where(y + k >= 4, ROWS, 0), 2 * ROWS, 0)
        first_pieces.append(lax.ppermute(pair, "y", ring(k)))
    second_pieces = [near, lax.ppermute(near, "x", ring(1)), lax.ppermute(near, "x", ring(2))]

    at = jnp.stack([4 * x + y, core]).astype(jnp.int32)
    lengths = doc_lengths[0]
    att0, dq0, self0, *pairs0 = attention(0, place_x_first, at, lengths, qm, qo, gm, go, *first_pieces)
    att1, dq1, self1, *pairs1 = attention(1, place_y_first, after(at, att0), lengths, qm, qo, gm, go, *second_pieces)

    sent0 = send_y(pairs0)
    sums0 = scatter_y(self0, after(sent0, self1), y)
    grad0 = scatter_x(sums0)
    sent1 = send_y(pairs1)
    sums1 = scatter_y(self1, sent1, y)
    grad1 = scatter_x(sums1)

    total = noted(near)
    total = total + lax.ppermute(after(total, att0), "x", ring(3))
    total = after(total + noted(second_pieces[1]) + noted(second_pieces[2]), sums1[1])
    pieces = [total] + [lax.ppermute(total, "dp", ring(k)) for k in (1, 2, 3)]
    total = jnp.concatenate(pieces, axis=0)

    own_grad = jnp.concatenate([grad0, grad1], axis=1).astype(BF)

    parts = [att0, att1, dq0, dq1]
    others = jnp.concatenate([part[HALF:] for part in parts], axis=1)
    others = lax.ppermute(after(others, sums1[1]), "core", SWAP)
    out_rows, dq_rows = finish(finish_rows, core, total, *parts, others, outs=2, width=QH * HD)
    got = lax.ppermute(own_grad[HALF:], "core", SWAP)
    key_grad, value_grad = finish(finish_keys, core, total, own_grad, got, outs=2, width=KVH * HD)
    return (out_rows[None], dq_rows[None], key_grad[None], value_grad[None])


def solution(mesh):
    split = Mesh(mesh.devices.reshape(4, 4, 4, 2), ("dp", "x", "y", "core"))
    ctx = ("x", "y", "core")
    rows = P("dp", ctx, None)
    return jax.shard_map(
        body,
        mesh=split,
        in_specs=(rows, rows, rows, rows, P("dp", ctx), P("dp", None)),
        out_specs=(rows, rows, rows, rows),
        check_vma=False,
    )
```

```python
import functools
import math

import jax
import jax.numpy as jnp
from jax import lax
from jax.experimental import pallas as pl
from jax.experimental.pallas import tpu as pltpu
from jax.sharding import Mesh, PartitionSpec as P

QH = 24
KVH = 4
HD = 128
CAP = 30.0
NEAR = 2
GROUP = QH // KVH
ROWS = 256
HALF = 128
WIDE = GROUP * ROWS
TILE = HALF
NOTE = 16
SLOTS = 9
BF = jnp.bfloat16
F32 = jnp.float32
SCALE = HD ** (-0.5)


def dot(a, b, over=(1, 0)):
    return lax.dot_general(a, b, (((over[0],), (over[1],)), ((), ())), preferred_element_type=F32)


def place_x_first(y):
    places = [(0, 0, 0), (1, 0, 4), (2, 0, 8)]
    for at, k in enumerate((1, 3, 2)):
        places += [(3 + at, 0, k), (3 + at, ROWS, 4 + k)]
    return places


def place_y_first(y):
    places = []
    for m in range(3):
        for at, k in enumerate((0, 1, 3, 2)):
            slot = 4 * m + k - jnp.where(y < k, 4, 0)
            places.append((m, at * (ROWS + NOTE), slot))
    return places


def attention_kernel(head, places_of, pieces, at_ref, len_ref, *refs):
    qm_ref, qo_ref, gm_ref, go_ref = refs[:4]
    piece_refs = refs[4:4 + pieces]
    att_ref, dq_ref, self_ref, *pair_refs = refs[4 + pieces:10 + pieces]
    keys, values, qs, gs, expo, slope, row_dot, dkv = refs[10 + pieces:]
    chip = at_ref[0]
    core = at_ref[1]
    row = lax.broadcasted_iota(jnp.int32, (HALF, 1), 0) + chip * ROWS
    row_pos = [row + core * HALF, row + (1 - core) * HALF]
    sub = lax.broadcasted_iota(jnp.int32, (1, ROWS), 1)
    key_off = sub + jnp.where(sub < HALF, core * HALF, (1 - core) * HALF - HALF)

    start = [jnp.zeros((HALF, 1), jnp.int32)] * 2
    low = jnp.int32(0)
    high = jnp.int32(0)
    edge = jnp.int32(0)
    for j in range(8):
        edge = edge + len_ref[j]
        start = [jnp.maximum(s, jnp.where(p >= edge, edge, 0)) for s, p in zip(start, row_pos)]
        low = jnp.maximum(low, jnp.where(chip * ROWS >= edge, edge, 0))
        high = jnp.maximum(high, jnp.where(chip * ROWS + ROWS - 1 >= edge, edge, 0))

    def needed(slot):
        return (slot <= chip) & ((chip - slot + 1) * ROWS > low)

    def block(slot):
        return pl.ds(pl.multiple_of(slot * ROWS, ROWS), ROWS)

    values[:, HD:] = jnp.ones((SLOTS * ROWS, HD), BF)
    for piece, first, slot in places_of(lax.rem(chip, 4)):
        @pl.when((slot >= 0) & (slot < SLOTS))
        def _():
            to = block(jnp.clip(slot, 0, SLOTS - 1))
            keys[to, :] = piece_refs[piece][first:first + ROWS, :HD]
            values[to, :HD] = piece_refs[piece][first:first + ROWS, HD:]

    for j in range(GROUP):
        cols = slice((head * GROUP + j) * HD, (head * GROUP + j + 1) * HD)
        for part, (q_in, g_in) in enumerate(((qm_ref, gm_ref), (qo_ref, go_ref))):
            rows = slice(j * ROWS + part * HALF, j * ROWS + (part + 1) * HALF)
            qs[rows, :] = q_in[:, cols]
            gs[rows, :] = g_in[:, cols]

    def forward(slot, masked):
        block_keys = keys[block(slot), :]
        for j in range(WIDE // TILE):
            rows = slice(j * TILE, (j + 1) * TILE)
            sq = jnp.tanh(dot(qs[rows, :], block_keys, (1, 1)) * (SCALE / CAP))
            e = jnp.exp2(sq * (CAP / math.log(2.0)))
            if masked:
                key_pos = (chip - slot) * ROWS + key_off
                e = jnp.where((key_pos >= start[j % 2]) & (key_pos <= row_pos[j % 2]), e, 0.0)
            expo[rows, block(slot)] = e.astype(BF)
            slope[rows, block(slot)] = (e * (1.0 - sq * sq)).astype(BF)

    def forward_step(slot, carry):
        plain = (slot > 0) & ((chip - slot) * ROWS >= high)

        @pl.when(needed(slot) & plain)
        def _():
            forward(slot, False)

        @pl.when(needed(slot) & jnp.logical_not(plain))
        def _():
            forward(slot, True)

        @pl.when(jnp.logical_not(needed(slot)))
        def _():
            expo[:, block(slot)] = jnp.zeros((WIDE, ROWS), BF)
            slope[:, block(slot)] = jnp.zeros((WIDE, ROWS), BF)

        return carry

    lax.fori_loop(0, SLOTS, forward_step, 0)

    for j in range(GROUP):
        rows = slice(j * ROWS, (j + 1) * ROWS)
        mixed = dot(expo[rows, :], values[...])
        inv = 1.0 / mixed[:, HD:]
        out = (mixed[:, :HD] * inv).astype(BF)
        att_ref[:, j * HD:(j + 1) * HD] = out
        g = (gs[rows, :].astype(F32) * inv).astype(BF)
        gs[rows, :] = g
        row_dot[rows, :] = jnp.broadcast_to(
            jnp.sum(g.astype(F32) * out.astype(F32), axis=1, keepdims=True), (ROWS, HD)
        )

    def backward(slot):
        block_values = values[block(slot), :HD]
        for j in range(WIDE // TILE):
            rows = slice(j * TILE, (j + 1) * TILE)
            dp = dot(gs[rows, :], block_values, (1, 1))
            rd = row_dot[rows, :]
            ds = slope[rows, block(slot)].astype(F32) * (dp - jnp.concatenate([rd, rd], axis=1))
            slope[rows, block(slot)] = ds.astype(BF)
        dkv[slot, :, :HD] = (dot(slope[:, block(slot)], qs[...], (0, 0)) * SCALE).astype(BF)
        dkv[slot, :, HD:] = dot(expo[:, block(slot)], gs[...], (0, 0)).astype(BF)

    def backward_step(slot, carry):
        @pl.when(needed(slot))
        def _():
            backward(slot)

        @pl.when(jnp.logical_not(needed(slot)))
        def _():
            dkv[slot] = jnp.zeros((ROWS, 2 * HD), BF)

        return carry

    lax.fori_loop(0, SLOTS, backward_step, 0)

    for j in range(GROUP):
        rows = slice(j * ROWS, (j + 1) * ROWS)
        dq_ref[:, j * HD:(j + 1) * HD] = (dot(slope[rows, :], keys[...]) * SCALE).astype(BF)
    for m in range(3):
        self_ref[m] = dkv[4 * m]
    for pair_ref, k in zip(pair_refs, (1, 3, 2)):
        pair_ref[:ROWS, :] = dkv[k]
        pair_ref[ROWS:, :] = dkv[4 + k]


def attention(head, places_of, at, lengths, qm, qo, gm, go, *pieces):
    smem = pl.BlockSpec(memory_space=pltpu.SMEM)
    vmem = pl.BlockSpec(memory_space=pltpu.VMEM)
    return pl.pallas_call(
        functools.partial(attention_kernel, head, places_of, len(pieces)),
        out_shape=(
            jax.ShapeDtypeStruct((ROWS, GROUP * HD), BF),
            jax.ShapeDtypeStruct((ROWS, GROUP * HD), BF),
            jax.ShapeDtypeStruct((3, ROWS, 2 * HD), BF),
        ) + (jax.ShapeDtypeStruct((2 * ROWS, 2 * HD), BF),) * 3,
        in_specs=[smem] * 2 + [vmem] * (4 + len(pieces)),
        out_specs=(vmem,) * 6,
        scratch_shapes=[
            pltpu.VMEM((SLOTS * ROWS, HD), BF),
            pltpu.VMEM((SLOTS * ROWS, 2 * HD), BF),
            pltpu.VMEM((WIDE, HD), BF),
            pltpu.VMEM((WIDE, HD), BF),
            pltpu.VMEM((WIDE, SLOTS * ROWS), BF),
            pltpu.VMEM((WIDE, SLOTS * ROWS), BF),
            pltpu.VMEM((WIDE, HD), F32),
            pltpu.VMEM((SLOTS, ROWS, 2 * HD), BF),
        ],
        compiler_params=pltpu.CompilerParams(vmem_limit_bytes=40 * 1024 * 1024),
        cost_estimate=pl.CostEstimate(
            flops=12 * WIDE * HD * ROWS * SLOTS * 4, bytes_accessed=6_000_000, transcendentals=7_000_000
        ),
    )(at, lengths, qm, qo, gm, go, *pieces)


def inverse(total_ref):
    total = jnp.sum(total_ref[...], axis=0, keepdims=True)
    return 1.0 / jnp.sum(total, axis=1, keepdims=True)


def finish_rows(core_ref, total_ref, att0, att1, dq0, dq1, others, out_ref, dq_ref):
    inv = inverse(total_ref)
    width = GROUP * HD
    for at, pair in ((0, (att0, att1)), (2, (dq0, dq1))):
        for to, mine in ((0, core_ref[0] == 0), (2 * width, core_ref[0] != 0)):
            for j, part in enumerate(pair):
                theirs = others[:, (at + j) * width:(at + j + 1) * width]
                rows = jnp.where(mine, part[:HALF, :], theirs)
                cols = slice(to + j * width, to + (j + 1) * width)
                if at == 0:
                    out_ref[:, cols] = rows
                else:
                    dq_ref[:, cols] = (rows.astype(F32) * inv).astype(BF)


def finish_keys(core_ref, total_ref, own, got, key_ref, value_ref):
    inv = inverse(total_ref)
    for to, mine in ((0, core_ref[0] == 0), (NEAR * HD, core_ref[0] != 0)):
        for h in range(NEAR):
            cols = slice(to + h * HD, to + (h + 1) * HD)
            for at, ref in ((2 * h * HD, key_ref), ((2 * h + 1) * HD, value_ref)):
                rows = jnp.where(mine, own[:HALF, at:at + HD], got[:, at:at + HD])
                ref[:, cols] = (rows.astype(F32) * inv).astype(BF)


def finish(kernel, core, *arrays, outs, width):
    vmem = pl.BlockSpec(memory_space=pltpu.VMEM)
    return pl.pallas_call(
        kernel,
        out_shape=(jax.ShapeDtypeStruct((HALF, width), BF),) * outs,
        in_specs=[pl.BlockSpec(memory_space=pltpu.SMEM)] + [vmem] * len(arrays),
        out_specs=(vmem,) * outs,
        compiler_params=pltpu.CompilerParams(vmem_limit_bytes=16 * 1024 * 1024),
    )(core.astype(jnp.int32).reshape(1), *arrays)


SWAP = [(0, 1), (1, 0)]


def ring(k):
    return [(i, (i + k) % 4) for i in range(4)]


def note(values):
    high = lax.reduce_precision(values, 8, 7)
    middle = lax.reduce_precision(values - high, 8, 7)
    rest = values - high - middle
    row = lax.broadcasted_iota(jnp.int32, (NOTE, HD), 0)
    parts = jnp.where(row == 0, high, jnp.where(row == 1, middle, jnp.where(row == 2, rest, 0.0)))
    return jnp.concatenate([parts, parts], axis=1).astype(BF)


def noted(array):
    return sum(array[at + ROWS:at + ROWS + 3, :HD].astype(F32) for at in range(0, 4 * (ROWS + NOTE), ROWS + NOTE))


def after(value, token):
    return lax.optimization_barrier((value, token))[0]


def send_y(pairs):
    return [lax.ppermute(pair, "y", ring(4 - k)) for pair, k in zip(pairs, (1, 3, 2))]


def scatter_y(selves, received, y):
    sums = [selves[m].astype(F32) for m in range(3)]
    for k, got in zip((1, 3, 2), received):
        got = got.astype(F32)
        over = y + k >= 4
        first, second = got[:ROWS], got[ROWS:]
        sums[0] = sums[0] + jnp.where(over, 0.0, first)
        sums[1] = sums[1] + jnp.where(over, first, second)
        sums[2] = sums[2] + jnp.where(over, second, 0.0)
    return sums[0], sums[1].astype(BF), sums[2].astype(BF)


def scatter_x(sums):
    t1 = lax.ppermute(sums[1], "x", ring(3))
    t2 = lax.ppermute(sums[2], "x", ring(2))
    return sums[0] + t1.astype(F32) + t2.astype(F32)


def body(queries, key_rows, value_rows, upstream, loss_weight, doc_lengths):
    x, y, core = lax.axis_index("x"), lax.axis_index("y"), lax.axis_index("core")
    weights_row = loss_weight[0]
    mine_at, other_at = core, 1 - core

    def half(array, at):
        size = array.shape[1] // 2
        return lax.dynamic_slice_in_dim(array, at * size, size, 1)

    def heads(at):
        k, v = half(key_rows[0], at), half(value_rows[0], at)
        return jnp.concatenate([k[:, :HD], v[:, :HD], k[:, HD:], v[:, HD:]], axis=1)

    weights = jnp.broadcast_to(weights_row[None], (8, HD))
    weights = weights + lax.ppermute(weights, "core", SWAP)
    kv_other = lax.ppermute(heads(other_at), "core", SWAP)
    own = jnp.concatenate([heads(mine_at), kv_other], axis=0)
    first = own[:, :2 * HD]
    second = jnp.concatenate([own[:, 2 * HD:], note(weights[:1])], axis=0)
    r1 = lax.ppermute(first, "x", ring(1))
    r2 = lax.ppermute(first, "x", ring(2))
    nearest = [lax.ppermute(second, "y", ring(k)) for k in (1, 3, 2)]

    weighted = (upstream[0].astype(F32) * weights_row[:, None]).astype(BF)
    qm, gm = half(queries[0], mine_at), half(weighted, mine_at)
    q_send, g_send = after((half(queries[0], other_at), half(weighted, other_at)), first)
    qo = lax.ppermute(q_send, "core", SWAP)
    go = lax.ppermute(g_send, "core", SWAP)

    three = jnp.concatenate([first, r1, r2], axis=0)
    three = after(three, (qo, go))
    first_pieces = [first, r1, r2]
    for k in (1, 3, 2):
        pair = lax.dynamic_slice_in_dim(three, jnp.where(y + k >= 4, ROWS, 0), 2 * ROWS, 0)
        first_pieces.append(lax.ppermute(pair, "y", ring(k)))
    near = jnp.concatenate([second] + nearest, axis=0)
    second_pieces = [near, lax.ppermute(near, "x", ring(1)), lax.ppermute(near, "x", ring(2))]

    at = jnp.stack([4 * x + y, core]).astype(jnp.int32)
    lengths = doc_lengths[0]
    att0, dq0, self0, *pairs0 = attention(0, place_x_first, at, lengths, qm, qo, gm, go, *first_pieces)
    att1, dq1, self1, *pairs1 = attention(1, place_y_first, after(at, att0), lengths, qm, qo, gm, go, *second_pieces)

    sent0 = send_y(pairs0)
    sums0 = scatter_y(self0, after(sent0, self1), y)
    grad0 = scatter_x(sums0)
    sent1 = send_y(pairs1)

    sums1 = scatter_y(self1, sent1, y)
    grad1 = scatter_x(sums1)

    total = noted(near)
    total = total + lax.ppermute(after(total, att0), "x", ring(3))
    total = after(total + noted(second_pieces[1]) + noted(second_pieces[2]), grad0)
    pieces = [total] + [lax.ppermute(total, "dp", ring(k)) for k in (1, 2, 3)]
    total = jnp.concatenate(pieces, axis=0)

    parts = [att0, att1, dq0, dq1]
    others = jnp.concatenate([part[HALF:] for part in parts], axis=1)
    others = lax.ppermute(after(others, sums1[1]), "core", SWAP)

    own_grad = jnp.concatenate([grad0, grad1], axis=1).astype(BF)

    out_rows, dq_rows = finish(finish_rows, core, total, *parts, others, outs=2, width=QH * HD)
    got = lax.ppermute(after(own_grad[HALF:], out_rows), "core", SWAP)
    key_grad, value_grad = finish(finish_keys, core, total, own_grad, got, outs=2, width=KVH * HD)
    return (out_rows[None], dq_rows[None], key_grad[None], value_grad[None])


def solution(mesh):
    split = Mesh(mesh.devices.reshape(4, 4, 4, 2), ("dp", "x", "y", "core"))
    ctx = ("x", "y", "core")
    rows = P("dp", ctx, None)
    return jax.shard_map(
        body,
        mesh=split,
        in_specs=(rows, rows, rows, rows, P("dp", ctx), P("dp", None)),
        out_specs=(rows, rows, rows, rows),
        check_vma=False,
    )
```

```python
import functools
import math

import jax
import jax.numpy as jnp
from jax import lax
from jax.experimental import pallas as pl
from jax.experimental.pallas import tpu as pltpu
from jax.sharding import Mesh, PartitionSpec as P

QH = 24
KVH = 4
HD = 128
CAP = 30.0
NEAR = 2
GROUP = QH // KVH
ROWS = 256
HALF = 128
WIDE = GROUP * ROWS
TILE = HALF
NOTE = 16
SLOTS = 9
BF = jnp.bfloat16
F32 = jnp.float32
SCALE = HD ** (-0.5)


def dot(a, b, over=(1, 0)):
    return lax.dot_general(a, b, (((over[0],), (over[1],)), ((), ())), preferred_element_type=F32)


def place_x_first(y):
    places = [(0, 0, 0), (1, 0, 4), (2, 0, 8)]
    for at, k in enumerate((1, 3, 2)):
        places += [(3 + at, 0, k), (3 + at, ROWS, 4 + k)]
    return places


def place_y_first(y):
    places = []
    for m in range(3):
        for at, k in enumerate((0, 1, 3, 2)):
            slot = 4 * m + k - jnp.where(y < k, 4, 0)
            places.append((m, at * (ROWS + NOTE), slot))
    return places


def attention_kernel(head, places_of, pieces, at_ref, len_ref, *refs):
    qm_ref, qo_ref, gm_ref, go_ref = refs[:4]
    piece_refs = refs[4:4 + pieces]
    att_ref, dq_ref, self_ref, *pair_refs = refs[4 + pieces:10 + pieces]
    keys, values, qs, gs, expo, slope, row_dot, dkv = refs[10 + pieces:]
    chip = at_ref[0]
    core = at_ref[1]
    row = lax.broadcasted_iota(jnp.int32, (HALF, 1), 0) + chip * ROWS
    row_pos = [row + core * HALF, row + (1 - core) * HALF]
    sub = lax.broadcasted_iota(jnp.int32, (1, ROWS), 1)
    key_off = sub + jnp.where(sub < HALF, core * HALF, (1 - core) * HALF - HALF)

    start = [jnp.zeros((HALF, 1), jnp.int32)] * 2
    low = jnp.int32(0)
    high = jnp.int32(0)
    edge = jnp.int32(0)
    for j in range(8):
        edge = edge + len_ref[j]
        start = [jnp.maximum(s, jnp.where(p >= edge, edge, 0)) for s, p in zip(start, row_pos)]
        low = jnp.maximum(low, jnp.where(chip * ROWS >= edge, edge, 0))
        high = jnp.maximum(high, jnp.where(chip * ROWS + ROWS - 1 >= edge, edge, 0))

    def needed(slot):
        return (slot <= chip) & ((chip - slot + 1) * ROWS > low)

    def block(slot):
        return pl.ds(pl.multiple_of(slot * ROWS, ROWS), ROWS)

    values[:, HD:] = jnp.ones((SLOTS * ROWS, HD), BF)
    for piece, first, slot in places_of(lax.rem(chip, 4)):
        @pl.when((slot >= 0) & (slot < SLOTS))
        def _():
            to = block(jnp.clip(slot, 0, SLOTS - 1))
            keys[to, :] = piece_refs[piece][first:first + ROWS, :HD]
            values[to, :HD] = piece_refs[piece][first:first + ROWS, HD:]

    for j in range(GROUP):
        cols = slice((head * GROUP + j) * HD, (head * GROUP + j + 1) * HD)
        for part, (q_in, g_in) in enumerate(((qm_ref, gm_ref), (qo_ref, go_ref))):
            rows = slice(j * ROWS + part * HALF, j * ROWS + (part + 1) * HALF)
            qs[rows, :] = q_in[:, cols]
            gs[rows, :] = g_in[:, cols]

    def forward(slot, masked):
        block_keys = keys[block(slot), :]
        for j in range(WIDE // TILE):
            rows = slice(j * TILE, (j + 1) * TILE)
            sq = jnp.tanh(dot(qs[rows, :], block_keys, (1, 1)) * (SCALE / CAP))
            e = jnp.exp2(sq * (CAP / math.log(2.0)))
            if masked:
                key_pos = (chip - slot) * ROWS + key_off
                e = jnp.where((key_pos >= start[j % 2]) & (key_pos <= row_pos[j % 2]), e, 0.0)
            expo[rows, block(slot)] = e.astype(BF)
            slope[rows, block(slot)] = (e * (1.0 - sq * sq)).astype(BF)

    def forward_step(slot, carry):
        plain = (slot > 0) & ((chip - slot) * ROWS >= high)

        @pl.when(needed(slot) & plain)
        def _():
            forward(slot, False)

        @pl.when(needed(slot) & jnp.logical_not(plain))
        def _():
            forward(slot, True)

        @pl.when(jnp.logical_not(needed(slot)))
        def _():
            expo[:, block(slot)] = jnp.zeros((WIDE, ROWS), BF)
            slope[:, block(slot)] = jnp.zeros((WIDE, ROWS), BF)

        return carry

    lax.fori_loop(0, SLOTS, forward_step, 0)

    for j in range(GROUP):
        rows = slice(j * ROWS, (j + 1) * ROWS)
        mixed = dot(expo[rows, :], values[...])
        inv = 1.0 / mixed[:, HD:]
        out = (mixed[:, :HD] * inv).astype(BF)
        att_ref[:, j * HD:(j + 1) * HD] = out
        g = (gs[rows, :].astype(F32) * inv).astype(BF)
        gs[rows, :] = g
        row_dot[rows, :] = jnp.broadcast_to(
            jnp.sum(g.astype(F32) * out.astype(F32), axis=1, keepdims=True), (ROWS, HD)
        )

    def backward(slot):
        block_values = values[block(slot), :HD]
        for j in range(WIDE // TILE):
            rows = slice(j * TILE, (j + 1) * TILE)
            dp = dot(gs[rows, :], block_values, (1, 1))
            rd = row_dot[rows, :]
            ds = slope[rows, block(slot)].astype(F32) * (dp - jnp.concatenate([rd, rd], axis=1))
            slope[rows, block(slot)] = ds.astype(BF)
        dkv[slot, :, :HD] = (dot(slope[:, block(slot)], qs[...], (0, 0)) * SCALE).astype(BF)
        dkv[slot, :, HD:] = dot(expo[:, block(slot)], gs[...], (0, 0)).astype(BF)

    def backward_step(slot, carry):
        @pl.when(needed(slot))
        def _():
            backward(slot)

        @pl.when(jnp.logical_not(needed(slot)))
        def _():
            dkv[slot] = jnp.zeros((ROWS, 2 * HD), BF)

        return carry

    lax.fori_loop(0, SLOTS, backward_step, 0)

    for j in range(GROUP):
        rows = slice(j * ROWS, (j + 1) * ROWS)
        dq_ref[:, j * HD:(j + 1) * HD] = (dot(slope[rows, :], keys[...]) * SCALE).astype(BF)
    for m in range(3):
        self_ref[m] = dkv[4 * m]
    for pair_ref, k in zip(pair_refs, (1, 3, 2)):
        pair_ref[:ROWS, :] = dkv[k]
        pair_ref[ROWS:, :] = dkv[4 + k]


def attention(head, places_of, at, lengths, qm, qo, gm, go, *pieces):
    smem = pl.BlockSpec(memory_space=pltpu.SMEM)
    vmem = pl.BlockSpec(memory_space=pltpu.VMEM)
    return pl.pallas_call(
        functools.partial(attention_kernel, head, places_of, len(pieces)),
        out_shape=(
            jax.ShapeDtypeStruct((ROWS, GROUP * HD), BF),
            jax.ShapeDtypeStruct((ROWS, GROUP * HD), BF),
            jax.ShapeDtypeStruct((3, ROWS, 2 * HD), BF),
        ) + (jax.ShapeDtypeStruct((2 * ROWS, 2 * HD), BF),) * 3,
        in_specs=[smem] * 2 + [vmem] * (4 + len(pieces)),
        out_specs=(vmem,) * 6,
        scratch_shapes=[
            pltpu.VMEM((SLOTS * ROWS, HD), BF),
            pltpu.VMEM((SLOTS * ROWS, 2 * HD), BF),
            pltpu.VMEM((WIDE, HD), BF),
            pltpu.VMEM((WIDE, HD), BF),
            pltpu.VMEM((WIDE, SLOTS * ROWS), BF),
            pltpu.VMEM((WIDE, SLOTS * ROWS), BF),
            pltpu.VMEM((WIDE, HD), F32),
            pltpu.VMEM((SLOTS, ROWS, 2 * HD), BF),
        ],
        compiler_params=pltpu.CompilerParams(vmem_limit_bytes=40 * 1024 * 1024),
        cost_estimate=pl.CostEstimate(
            flops=12 * WIDE * HD * ROWS * SLOTS * 4, bytes_accessed=6_000_000, transcendentals=7_000_000
        ),
    )(at, lengths, qm, qo, gm, go, *pieces)


def inverse(total_ref):
    total = jnp.sum(total_ref[...], axis=0, keepdims=True)
    return 1.0 / jnp.sum(total, axis=1, keepdims=True)


def finish_rows(core_ref, total_ref, att0, att1, dq0, dq1, others, out_ref, dq_ref):
    inv = inverse(total_ref)
    width = GROUP * HD
    for at, pair in ((0, (att0, att1)), (2, (dq0, dq1))):
        for to, mine in ((0, core_ref[0] == 0), (2 * width, core_ref[0] != 0)):
            for j, part in enumerate(pair):
                theirs = others[:, (at + j) * width:(at + j + 1) * width]
                rows = jnp.where(mine, part[:HALF, :], theirs)
                cols = slice(to + j * width, to + (j + 1) * width)
                if at == 0:
                    out_ref[:, cols] = rows
                else:
                    dq_ref[:, cols] = (rows.astype(F32) * inv).astype(BF)


def finish_keys(core_ref, total_ref, own, got, key_ref, value_ref):
    inv = inverse(total_ref)
    for to, mine in ((0, core_ref[0] == 0), (NEAR * HD, core_ref[0] != 0)):
        for h in range(NEAR):
            cols = slice(to + h * HD, to + (h + 1) * HD)
            for at, ref in ((2 * h * HD, key_ref), ((2 * h + 1) * HD, value_ref)):
                rows = jnp.where(mine, own[:HALF, at:at + HD], got[:, at:at + HD])
                ref[:, cols] = (rows.astype(F32) * inv).astype(BF)


def finish(kernel, core, *arrays, outs, width):
    vmem = pl.BlockSpec(memory_space=pltpu.VMEM)
    return pl.pallas_call(
        kernel,
        out_shape=(jax.ShapeDtypeStruct((HALF, width), BF),) * outs,
        in_specs=[pl.BlockSpec(memory_space=pltpu.SMEM)] + [vmem] * len(arrays),
        out_specs=(vmem,) * outs,
        compiler_params=pltpu.CompilerParams(vmem_limit_bytes=16 * 1024 * 1024),
    )(core.astype(jnp.int32).reshape(1), *arrays)


SWAP = [(0, 1), (1, 0)]


def ring(k):
    return [(i, (i + k) % 4) for i in range(4)]


def note(values):
    high = lax.reduce_precision(values, 8, 7)
    middle = lax.reduce_precision(values - high, 8, 7)
    rest = values - high - middle
    row = lax.broadcasted_iota(jnp.int32, (NOTE, HD), 0)
    parts = jnp.where(row == 0, high, jnp.where(row == 1, middle, jnp.where(row == 2, rest, 0.0)))
    return jnp.concatenate([parts, parts], axis=1).astype(BF)


def noted(array):
    return sum(array[at + ROWS:at + ROWS + 3, :HD].astype(F32) for at in range(0, 4 * (ROWS + NOTE), ROWS + NOTE))


def after(value, token):
    return lax.optimization_barrier((value, token))[0]


def send_y(pairs):
    return [lax.ppermute(pair, "y", ring(4 - k)) for pair, k in zip(pairs, (1, 3, 2))]


def scatter_y(selves, received, y):
    sums = [selves[m].astype(F32) for m in range(3)]
    for k, got in zip((1, 3, 2), received):
        got = got.astype(F32)
        over = y + k >= 4
        first, second = got[:ROWS], got[ROWS:]
        sums[0] = sums[0] + jnp.where(over, 0.0, first)
        sums[1] = sums[1] + jnp.where(over, first, second)
        sums[2] = sums[2] + jnp.where(over, second, 0.0)
    return sums[0], sums[1].astype(BF), sums[2].astype(BF)


def scatter_x(sums):
    t1 = lax.ppermute(sums[1], "x", ring(3))
    t2 = lax.ppermute(sums[2], "x", ring(2))
    return sums[0] + t1.astype(F32) + t2.astype(F32)


def body(queries, key_rows, value_rows, upstream, loss_weight, doc_lengths):
    x, y, core = lax.axis_index("x"), lax.axis_index("y"), lax.axis_index("core")
    weights_row = loss_weight[0]
    mine_at, other_at = core, 1 - core

    def half(array, at):
        size = array.shape[1] // 2
        return lax.dynamic_slice_in_dim(array, at * size, size, 1)

    def heads(at):
        k, v = half(key_rows[0], at), half(value_rows[0], at)
        return jnp.concatenate([k[:, :HD], v[:, :HD], k[:, HD:], v[:, HD:]], axis=1)

    weights = jnp.broadcast_to(weights_row[None], (8, HD))
    weights = weights + lax.ppermute(weights, "core", SWAP)
    kv_other = lax.ppermute(heads(other_at), "core", SWAP)
    own = jnp.concatenate([heads(mine_at), kv_other], axis=0)
    first = own[:, :2 * HD]
    second = jnp.concatenate([own[:, 2 * HD:], note(weights[:1])], axis=0)
    r1 = lax.ppermute(first, "x", ring(1))
    r2 = lax.ppermute(first, "x", ring(2))
    nearest = [lax.ppermute(second, "y", ring(k)) for k in (1, 3, 2)]

    weighted = (upstream[0].astype(F32) * weights_row[:, None]).astype(BF)
    qm, gm = half(queries[0], mine_at), half(weighted, mine_at)
    q_send, g_send = after((half(queries[0], other_at), half(weighted, other_at)), first)
    qo = lax.ppermute(q_send, "core", SWAP)
    go = lax.ppermute(g_send, "core", SWAP)

    three = jnp.concatenate([first, r1, r2], axis=0)
    three = after(three, (qo, go))
    first_pieces = [first, r1, r2]
    for k in (1, 3, 2):
        pair = lax.dynamic_slice_in_dim(three, jnp.where(y + k >= 4, ROWS, 0), 2 * ROWS, 0)
        first_pieces.append(lax.ppermute(pair, "y", ring(k)))
    near = jnp.concatenate([second] + nearest, axis=0)
    second_pieces = [near, lax.ppermute(near, "x", ring(1)), lax.ppermute(near, "x", ring(2))]

    at = jnp.stack([4 * x + y, core]).astype(jnp.int32)
    lengths = doc_lengths[0]
    att0, dq0, self0, *pairs0 = attention(0, place_x_first, at, lengths, qm, qo, gm, go, *first_pieces)
    att1, dq1, self1, *pairs1 = attention(1, place_y_first, after(at, att0), lengths, qm, qo, gm, go, *second_pieces)

    sent0 = send_y(pairs0)
    sums0 = scatter_y(self0, after(sent0, self1), y)
    grad0 = scatter_x(sums0)
    sent1 = send_y(pairs1)

    sums1 = scatter_y(self1, sent1, y)
    grad1 = scatter_x(sums1)

    total = noted(near)
    total = total + lax.ppermute(after(total, sums0[1]), "x", ring(3))
    total = after(total + noted(second_pieces[1]) + noted(second_pieces[2]), grad0)
    pieces = [total] + [lax.ppermute(total, "dp", ring(k)) for k in (1, 2, 3)]
    total = jnp.concatenate(pieces, axis=0)

    parts = [att0, att1, dq0, dq1]
    others = jnp.concatenate([part[HALF:] for part in parts], axis=1)
    others = lax.ppermute(after(others, sums1[1]), "core", SWAP)

    own_grad = jnp.concatenate([grad0, after(grad1, total)], axis=1).astype(BF)

    out_rows, dq_rows = finish(finish_rows, core, total, *parts, others, outs=2, width=QH * HD)
    got = after(lax.ppermute(own_grad[HALF:], "core", SWAP), out_rows)
    key_grad, value_grad = finish(finish_keys, core, total, own_grad, got, outs=2, width=KVH * HD)
    return (out_rows[None], dq_rows[None], key_grad[None], value_grad[None])


def solution(mesh):
    split = Mesh(mesh.devices.reshape(4, 4, 4, 2), ("dp", "x", "y", "core"))
    ctx = ("x", "y", "core")
    rows = P("dp", ctx, None)
    return jax.shard_map(
        body,
        mesh=split,
        in_specs=(rows, rows, rows, rows, P("dp", ctx), P("dp", None)),
        out_specs=(rows, rows, rows, rows),
        check_vma=False,
    )
```

```python
import functools
import math

import jax
import jax.numpy as jnp
from jax import lax
from jax.experimental import pallas as pl
from jax.experimental.pallas import tpu as pltpu
from jax.sharding import Mesh, PartitionSpec as P

QH = 24
KVH = 4
HD = 128
CAP = 30.0
NEAR = 2
GROUP = QH // KVH
ROWS = 256
HALF = 128
WIDE = GROUP * ROWS
TILE = HALF
NOTE = 16
SLOTS = 9
BF = jnp.bfloat16
F32 = jnp.float32
SCALE = HD ** (-0.5)


def dot(a, b, over=(1, 0)):
    return lax.dot_general(a, b, (((over[0],), (over[1],)), ((), ())), preferred_element_type=F32)


def place_x_first(y):
    places = [(0, 0, 0), (1, 0, 4), (2, 0, 8)]
    for at, k in enumerate((1, 3, 2)):
        places += [(3 + at, 0, k), (3 + at, ROWS, 4 + k)]
    return places


def place_y_first(y):
    places = []
    for m in range(3):
        for at, k in enumerate((0, 1, 3, 2)):
            slot = 4 * m + k - jnp.where(y < k, 4, 0)
            places.append((m, at * (ROWS + NOTE), slot))
    return places


def attention_kernel(head, places_of, pieces, at_ref, len_ref, *refs):
    qm_ref, qo_ref, gm_ref, go_ref = refs[:4]
    piece_refs = refs[4:4 + pieces]
    att_ref, dq_ref, self_ref, *pair_refs = refs[4 + pieces:10 + pieces]
    keys, values, qs, gs, expo, slope, row_dot, dkv = refs[10 + pieces:]
    chip = at_ref[0]
    core = at_ref[1]
    row = lax.broadcasted_iota(jnp.int32, (HALF, 1), 0) + chip * ROWS
    row_pos = [row + core * HALF, row + (1 - core) * HALF]
    sub = lax.broadcasted_iota(jnp.int32, (1, ROWS), 1)
    key_off = sub + jnp.where(sub < HALF, core * HALF, (1 - core) * HALF - HALF)

    start = [jnp.zeros((HALF, 1), jnp.int32)] * 2
    low = jnp.int32(0)
    high = jnp.int32(0)
    edge = jnp.int32(0)
    for j in range(8):
        edge = edge + len_ref[j]
        start = [jnp.maximum(s, jnp.where(p >= edge, edge, 0)) for s, p in zip(start, row_pos)]
        low = jnp.maximum(low, jnp.where(chip * ROWS >= edge, edge, 0))
        high = jnp.maximum(high, jnp.where(chip * ROWS + ROWS - 1 >= edge, edge, 0))

    def needed(slot):
        return (slot <= chip) & ((chip - slot + 1) * ROWS > low)

    def block(slot):
        return pl.ds(pl.multiple_of(slot * ROWS, ROWS), ROWS)

    values[:, HD:] = jnp.ones((SLOTS * ROWS, HD), BF)
    for piece, first, slot in places_of(lax.rem(chip, 4)):
        @pl.when((slot >= 0) & (slot < SLOTS))
        def _():
            to = block(jnp.clip(slot, 0, SLOTS - 1))
            keys[to, :] = piece_refs[piece][first:first + ROWS, :HD]
            values[to, :HD] = piece_refs[piece][first:first + ROWS, HD:]

    for j in range(GROUP):
        cols = slice((head * GROUP + j) * HD, (head * GROUP + j + 1) * HD)
        for part, (q_in, g_in) in enumerate(((qm_ref, gm_ref), (qo_ref, go_ref))):
            rows = slice(j * ROWS + part * HALF, j * ROWS + (part + 1) * HALF)
            qs[rows, :] = q_in[:, cols]
            gs[rows, :] = g_in[:, cols]

    def forward(slot, masked):
        block_keys = keys[block(slot), :]
        for j in range(WIDE // TILE):
            rows = slice(j * TILE, (j + 1) * TILE)
            sq = jnp.tanh(dot(qs[rows, :], block_keys, (1, 1)) * (SCALE / CAP))
            e = jnp.exp2(sq * (CAP / math.log(2.0)))
            if masked:
                key_pos = (chip - slot) * ROWS + key_off
                e = jnp.where((key_pos >= start[j % 2]) & (key_pos <= row_pos[j % 2]), e, 0.0)
            expo[rows, block(slot)] = e.astype(BF)
            slope[rows, block(slot)] = (e * (1.0 - sq * sq)).astype(BF)

    def forward_step(slot, carry):
        plain = (slot > 0) & ((chip - slot) * ROWS >= high)

        @pl.when(needed(slot) & plain)
        def _():
            forward(slot, False)

        @pl.when(needed(slot) & jnp.logical_not(plain))
        def _():
            forward(slot, True)

        @pl.when(jnp.logical_not(needed(slot)))
        def _():
            expo[:, block(slot)] = jnp.zeros((WIDE, ROWS), BF)
            slope[:, block(slot)] = jnp.zeros((WIDE, ROWS), BF)

        return carry

    lax.fori_loop(0, SLOTS, forward_step, 0)

    for j in range(GROUP):
        rows = slice(j * ROWS, (j + 1) * ROWS)
        mixed = dot(expo[rows, :], values[...])
        inv = 1.0 / mixed[:, HD:]
        out = (mixed[:, :HD] * inv).astype(BF)
        att_ref[:, j * HD:(j + 1) * HD] = out
        g = (gs[rows, :].astype(F32) * inv).astype(BF)
        gs[rows, :] = g
        row_dot[rows, :] = jnp.broadcast_to(
            jnp.sum(g.astype(F32) * out.astype(F32), axis=1, keepdims=True), (ROWS, HD)
        )

    def backward(slot):
        block_values = values[block(slot), :HD]
        for j in range(WIDE // TILE):
            rows = slice(j * TILE, (j + 1) * TILE)
            dp = dot(gs[rows, :], block_values, (1, 1))
            rd = row_dot[rows, :]
            ds = slope[rows, block(slot)].astype(F32) * (dp - jnp.concatenate([rd, rd], axis=1))
            slope[rows, block(slot)] = ds.astype(BF)
        dkv[slot, :, :HD] = (dot(slope[:, block(slot)], qs[...], (0, 0)) * SCALE).astype(BF)
        dkv[slot, :, HD:] = dot(expo[:, block(slot)], gs[...], (0, 0)).astype(BF)

    def backward_step(slot, carry):
        @pl.when(needed(slot))
        def _():
            backward(slot)

        @pl.when(jnp.logical_not(needed(slot)))
        def _():
            dkv[slot] = jnp.zeros((ROWS, 2 * HD), BF)

        return carry

    lax.fori_loop(0, SLOTS, backward_step, 0)

    for j in range(GROUP):
        rows = slice(j * ROWS, (j + 1) * ROWS)
        dq_ref[:, j * HD:(j + 1) * HD] = (dot(slope[rows, :], keys[...]) * SCALE).astype(BF)
    for m in range(3):
        self_ref[m] = dkv[4 * m]
    for pair_ref, k in zip(pair_refs, (1, 3, 2)):
        pair_ref[:ROWS, :] = dkv[k]
        pair_ref[ROWS:, :] = dkv[4 + k]


def attention(head, places_of, at, lengths, qm, qo, gm, go, *pieces):
    smem = pl.BlockSpec(memory_space=pltpu.SMEM)
    vmem = pl.BlockSpec(memory_space=pltpu.VMEM)
    return pl.pallas_call(
        functools.partial(attention_kernel, head, places_of, len(pieces)),
        out_shape=(
            jax.ShapeDtypeStruct((ROWS, GROUP * HD), BF),
            jax.ShapeDtypeStruct((ROWS, GROUP * HD), BF),
            jax.ShapeDtypeStruct((3, ROWS, 2 * HD), BF),
        ) + (jax.ShapeDtypeStruct((2 * ROWS, 2 * HD), BF),) * 3,
        in_specs=[smem] * 2 + [vmem] * (4 + len(pieces)),
        out_specs=(vmem,) * 6,
        scratch_shapes=[
            pltpu.VMEM((SLOTS * ROWS, HD), BF),
            pltpu.VMEM((SLOTS * ROWS, 2 * HD), BF),
            pltpu.VMEM((WIDE, HD), BF),
            pltpu.VMEM((WIDE, HD), BF),
            pltpu.VMEM((WIDE, SLOTS * ROWS), BF),
            pltpu.VMEM((WIDE, SLOTS * ROWS), BF),
            pltpu.VMEM((WIDE, HD), F32),
            pltpu.VMEM((SLOTS, ROWS, 2 * HD), BF),
        ],
        compiler_params=pltpu.CompilerParams(vmem_limit_bytes=40 * 1024 * 1024),
        cost_estimate=pl.CostEstimate(
            flops=12 * WIDE * HD * ROWS * SLOTS * 4, bytes_accessed=6_000_000, transcendentals=7_000_000
        ),
    )(at, lengths, qm, qo, gm, go, *pieces)


def inverse(total_ref):
    total = jnp.sum(total_ref[...], axis=0, keepdims=True)
    return 1.0 / jnp.sum(total, axis=1, keepdims=True)


def finish_rows(core_ref, total_ref, att0, att1, dq0, dq1, others, out_ref, dq_ref):
    inv = inverse(total_ref)
    width = GROUP * HD
    for at, pair in ((0, (att0, att1)), (2, (dq0, dq1))):
        for to, mine in ((0, core_ref[0] == 0), (2 * width, core_ref[0] != 0)):
            for j, part in enumerate(pair):
                theirs = others[:, (at + j) * width:(at + j + 1) * width]
                rows = jnp.where(mine, part[:HALF, :], theirs)
                cols = slice(to + j * width, to + (j + 1) * width)
                if at == 0:
                    out_ref[:, cols] = rows
                else:
                    dq_ref[:, cols] = (rows.astype(F32) * inv).astype(BF)


def finish_keys(core_ref, total_ref, own, got, key_ref, value_ref):
    inv = inverse(total_ref)
    for to, mine in ((0, core_ref[0] == 0), (NEAR * HD, core_ref[0] != 0)):
        for h in range(NEAR):
            cols = slice(to + h * HD, to + (h + 1) * HD)
            for at, ref in ((2 * h * HD, key_ref), ((2 * h + 1) * HD, value_ref)):
                rows = jnp.where(mine, own[:HALF, at:at + HD], got[:, at:at + HD])
                ref[:, cols] = (rows.astype(F32) * inv).astype(BF)


def finish(kernel, core, *arrays, outs, width):
    vmem = pl.BlockSpec(memory_space=pltpu.VMEM)
    return pl.pallas_call(
        kernel,
        out_shape=(jax.ShapeDtypeStruct((HALF, width), BF),) * outs,
        in_specs=[pl.BlockSpec(memory_space=pltpu.SMEM)] + [vmem] * len(arrays),
        out_specs=(vmem,) * outs,
        compiler_params=pltpu.CompilerParams(vmem_limit_bytes=16 * 1024 * 1024),
    )(core.astype(jnp.int32).reshape(1), *arrays)


SWAP = [(0, 1), (1, 0)]


def ring(k):
    return [(i, (i + k) % 4) for i in range(4)]


def note(values):
    high = lax.reduce_precision(values, 8, 7)
    middle = lax.reduce_precision(values - high, 8, 7)
    rest = values - high - middle
    row = lax.broadcasted_iota(jnp.int32, (NOTE, HD), 0)
    parts = jnp.where(row == 0, high, jnp.where(row == 1, middle, jnp.where(row == 2, rest, 0.0)))
    return jnp.concatenate([parts, parts], axis=1).astype(BF)


def noted(array):
    return sum(array[at + ROWS:at + ROWS + 3, :HD].astype(F32) for at in range(0, 4 * (ROWS + NOTE), ROWS + NOTE))


def after(value, token):
    return lax.optimization_barrier((value, token))[0]


def send_y(pairs):
    return [lax.ppermute(pair, "y", ring(4 - k)) for pair, k in zip(pairs, (1, 3, 2))]


def scatter_y(selves, received, y):
    sums = [selves[m].astype(F32) for m in range(3)]
    for k, got in zip((1, 3, 2), received):
        got = got.astype(F32)
        over = y + k >= 4
        first, second = got[:ROWS], got[ROWS:]
        sums[0] = sums[0] + jnp.where(over, 0.0, first)
        sums[1] = sums[1] + jnp.where(over, first, second)
        sums[2] = sums[2] + jnp.where(over, second, 0.0)
    return sums[0], sums[1].astype(BF), sums[2].astype(BF)


def scatter_x(sums):
    t1 = lax.ppermute(sums[1], "x", ring(3))
    t2 = lax.ppermute(sums[2], "x", ring(2))
    return sums[0] + t1.astype(F32) + t2.astype(F32)


def body(queries, key_rows, value_rows, upstream, loss_weight, doc_lengths):
    x, y, core = lax.axis_index("x"), lax.axis_index("y"), lax.axis_index("core")
    weights_row = loss_weight[0]
    mine_at, other_at = core, 1 - core

    def half(array, at):
        size = array.shape[1] // 2
        return lax.dynamic_slice_in_dim(array, at * size, size, 1)

    def heads(at):
        k, v = half(key_rows[0], at), half(value_rows[0], at)
        return jnp.concatenate([k[:, :HD], v[:, :HD], k[:, HD:], v[:, HD:]], axis=1)

    weights = loss_weight + lax.ppermute(loss_weight, "core", SWAP)
    kv_other = lax.ppermute(heads(other_at), "core", SWAP)
    own = jnp.concatenate([heads(mine_at), kv_other], axis=0)
    first = own[:, :2 * HD]
    second = jnp.concatenate([own[:, 2 * HD:], note(weights)], axis=0)
    r1 = lax.ppermute(first, "x", ring(1))
    r2 = lax.ppermute(first, "x", ring(2))
    nearest = [lax.ppermute(second, "y", ring(k)) for k in (1, 3, 2)]

    weighted = (upstream[0].astype(F32) * weights_row[:, None]).astype(BF)
    qm, gm = half(queries[0], mine_at), half(weighted, mine_at)
    q_send, g_send = after((half(queries[0], other_at), half(weighted, other_at)), first)
    qo = lax.ppermute(q_send, "core", SWAP)
    go = lax.ppermute(g_send, "core", SWAP)

    three = jnp.concatenate([first, r1, r2], axis=0)
    three = after(three, (qo, go))
    first_pieces = [first, r1, r2]
    for k in (1, 3, 2):
        pair = lax.dynamic_slice_in_dim(three, jnp.where(y + k >= 4, ROWS, 0), 2 * ROWS, 0)
        first_pieces.append(lax.ppermute(pair, "y", ring(k)))
    near = jnp.concatenate([second] + nearest, axis=0)
    second_pieces = [near, lax.ppermute(near, "x", ring(1)), lax.ppermute(near, "x", ring(2))]

    at = jnp.stack([4 * x + y, core]).astype(jnp.int32)
    lengths = doc_lengths[0]
    att0, dq0, self0, *pairs0 = attention(0, place_x_first, at, lengths, qm, qo, gm, go, *first_pieces)
    att1, dq1, self1, *pairs1 = attention(1, place_y_first, after(at, att0), lengths, qm, qo, gm, go, *second_pieces)

    sent0 = send_y(pairs0)
    sums0 = scatter_y(self0, after(sent0, self1), y)
    grad0 = scatter_x(sums0)
    sent1 = send_y(pairs1)

    sums1 = scatter_y(self1, sent1, y)
    grad1 = scatter_x(sums1)

    total = noted(near)
    total = total + lax.ppermute(after(total, sums0[1]), "x", ring(3))
    total = after(total + noted(second_pieces[1]) + noted(second_pieces[2]), grad0)
    pieces = [total] + [lax.ppermute(total, "dp", ring(k)) for k in (1, 2, 3)]
    total = jnp.concatenate(pieces, axis=0)

    parts = [att0, att1, dq0, dq1]
    others = jnp.concatenate([part[HALF:] for part in parts], axis=1)
    others = lax.ppermute(after(others, sums1[1]), "core", SWAP)

    own_grad = jnp.concatenate([grad0, after(grad1, total)], axis=1).astype(BF)

    out_rows, dq_rows = finish(finish_rows, core, total, *parts, others, outs=2, width=QH * HD)
    got = after(lax.ppermute(own_grad[HALF:], "core", SWAP), out_rows)
    key_grad, value_grad = finish(finish_keys, core, total, own_grad, got, outs=2, width=KVH * HD)
    return (out_rows[None], dq_rows[None], key_grad[None], value_grad[None])


def solution(mesh):
    split = Mesh(mesh.devices.reshape(4, 4, 4, 2), ("dp", "x", "y", "core"))
    ctx = ("x", "y", "core")
    rows = P("dp", ctx, None)
    return jax.shard_map(
        body,
        mesh=split,
        in_specs=(rows, rows, rows, rows, P("dp", ctx), P("dp", None)),
        out_specs=(rows, rows, rows, rows),
        check_vma=False,
    )
```
